32 devices in a mesh: dp: 2 (over x), node: 4 (over z), local: 4 (over y, core).
Axes of the slice: x: 2, y: 2, z: 4, core: 2. Of those that a mesh axis runs over, the one named last changes fastest.
Arguments:
- tokens_in: bfloat16 [2, 4, 64, 4, 3584], P('dp', 'node'), may hold values from -6 to 6
- grad_rows: bfloat16 [2, 4, 64, 4, 3584], P('dp', 'node'), may hold values from -6 to 6
- combine_weights: float32 [2, 4, 64, 4], P('dp', 'node'), may hold values from 0.05 to 1
- live_counts: int32 [2, 4, 4], P('dp', 'node'), may hold values from 0 to 64, as said below
- w_gate: bfloat16 [4, 3584, 2048], P('node', None, 'local'), may hold values from -0.09375 to 0.09375
- w_up: bfloat16 [4, 3584, 2048], P('node', None, 'local'), may hold values from -0.09375 to 0.09375
- w_down: bfloat16 [4, 3584, 2048], P('node', None, 'local'), may hold values from -0.125 to 0.125
Outputs:
- d_tokens: bfloat16 [2, 4, 64, 4, 3584], P('dp', 'node', 'local')
- grad_gate: bfloat16 [4, 3584, 2048], P('node', 'dp', 'local')
- grad_up: bfloat16 [4, 3584, 2048], P('node', 'dp', 'local')
- grad_down: bfloat16 [4, 3584, 2048], P('node', 'dp', 'local')
The draws below stay inside these ranges and needn't reach their ends.
Inputs may be any that keep to these rules, and one draw needn't show every extreme that they name: `live_counts`: each replica has some source and expert pair with all 64 slots live; loads differ strongly between experts.
All inputs are finite; a program needn't handle non-finite values.
Results may differ from the reference program's by a relative error of at most 0.019.
Values may be sent and summed in bfloat16 or wider, within the bound.
No kernel may reach another device: no remote copies, remote signals or barrier semaphores. Data moves between devices by JAX's collectives and lax.ppermute only.
A program may use at most 128 MiB of HBM per device.

```python
import math
import jax
import jax.numpy as jnp
from jax import lax

D = 3584
HID = 2048
SLOTS = 64
REPLICAS = 2
NODES = 4


def draw_live_counts(key, part):
    key_hot = jax.random.fold_in(key, 11)
    key_base = jax.random.fold_in(key, 12)
    key_pick = jax.random.fold_in(key, 13)
    hotness = jax.random.randint(key_hot, (REPLICAS, NODES, 1), 1, 5)
    base_load = jax.random.randint(key_base, (REPLICAS, NODES, NODES), 0, SLOTS // 3 + 2)
    loads = jnp.minimum(base_load * hotness, SLOTS).reshape(REPLICAS, NODES * NODES)
    picked = jax.random.randint(key_pick, (REPLICAS,), 0, NODES * NODES)
    chosen = jnp.arange(NODES * NODES, dtype=jnp.int32)[None, :] == picked[:, None]
    loads = jnp.where(chosen, SLOTS, loads)
    return loads.reshape(REPLICAS, NODES, NODES).astype(jnp.int32)


def levels(stream_key, shape, cuts, low, high):
    loudness = 1.0
    for axis_at, shards_of in cuts:
        draws = jax.random.uniform(jax.random.fold_in(jax.random.fold_in(stream_key, 6), axis_at), (shards_of,), jnp.float32, low / len(cuts), high / len(cuts))
        loudness = loudness * jnp.repeat(jnp.exp(draws), shape[axis_at] // shards_of).reshape((-1,) + (1,) * (len(shape) - 1 - axis_at))
    return loudness


def gaussian(stream_key, dims, width, limit, split=(), kind=jnp.bfloat16):
    drawn = width * jax.random.normal(stream_key, dims, jnp.float32)
    if split:
        drawn = drawn * levels(stream_key, dims, split, -0.22, 0.18)
    return jnp.clip(drawn, -limit, limit).astype(kind)


def setup_inputs(seed: int = 0) -> dict:
    splits = jax.random.split(jax.random.key(seed), 8)
    return {
        "tokens_in": gaussian(splits[0], (REPLICAS, NODES, SLOTS, NODES, D), 1.0, 6.0, ((0, 2), (1, 4))),
        "grad_rows": gaussian(splits[1], (REPLICAS, NODES, SLOTS, NODES, D), 1.0, 6.0, ((0, 2), (1, 4))),
        "combine_weights": jnp.clip(jnp.exp(math.log(1.0) - 2.9957323 * jax.random.uniform(splits[2], (REPLICAS, NODES, SLOTS, NODES), jnp.float32) ** levels(splits[2], (REPLICAS, NODES, SLOTS, NODES), ((0, 2), (1, 4)), -0.2, 0.2)), 0.05, 1.0),
        "live_counts": draw_live_counts(jax.random.fold_in(splits[7], 71), 0),
        "w_gate": gaussian(splits[4], (NODES, D, HID), D ** -0.5, 0.09375, ((0, 4), (2, 4))),
        "w_up": gaussian(splits[5], (NODES, D, HID), D ** -0.5, 0.09375, ((0, 4), (2, 4))),
        "w_down": gaussian(splits[6], (NODES, D, HID), HID ** -0.5, 0.125, ((0, 4), (2, 4))),
    }


def expert_pass(token_block, grad_block, weight_block, count_row, gate_weight, up_weight, down_weight):
    live_mask = (jnp.arange(SLOTS, dtype=jnp.int32)[:, None] < count_row[None, :]).astype(jnp.float32)
    scaled_rows = (grad_block.astype(jnp.float32) * (weight_block * live_mask)[:, :, None]).astype(jnp.bfloat16)
    scaled_rows = scaled_rows.reshape(SLOTS * NODES, D)
    flat_tokens = token_block.reshape(SLOTS * NODES, D)
    gate_pre = jnp.dot(flat_tokens, gate_weight, preferred_element_type=jnp.float32)
    up_pre = jnp.dot(flat_tokens, up_weight, preferred_element_type=jnp.float32)
    sigmoid_gate = jax.nn.sigmoid(gate_pre)
    activated = gate_pre * sigmoid_gate
    hidden = (activated * up_pre).astype(jnp.bfloat16)
    hidden_grad = jnp.dot(scaled_rows, down_weight, preferred_element_type=jnp.float32)
    gate_grad = (hidden_grad * up_pre * sigmoid_gate * (1.0 + gate_pre * (1.0 - sigmoid_gate))).astype(jnp.bfloat16)
    up_grad = (hidden_grad * activated).astype(jnp.bfloat16)
    input_grad = jnp.dot(gate_grad, gate_weight.T, preferred_element_type=jnp.float32) + jnp.dot(up_grad, up_weight.T, preferred_element_type=jnp.float32)
    gate_part = jnp.dot(flat_tokens.T, gate_grad, preferred_element_type=jnp.float32).astype(jnp.bfloat16)
    up_part = jnp.dot(flat_tokens.T, up_grad, preferred_element_type=jnp.float32).astype(jnp.bfloat16)
    down_part = jnp.dot(scaled_rows.T, hidden, preferred_element_type=jnp.float32).astype(jnp.bfloat16)
    return input_grad.astype(jnp.bfloat16).reshape(SLOTS, NODES, D), gate_part, up_part, down_part


def reference(tokens_in, grad_rows, combine_weights, live_counts, w_gate, w_up, w_down):
    def per_expert(expert):
        gate_weight = w_gate[expert]
        up_weight = w_up[expert]
        down_weight = w_down[expert]
        inputs_list = []
        gate_total = jnp.zeros((D, HID), jnp.float32)
        up_total = jnp.zeros((D, HID), jnp.float32)
        down_total = jnp.zeros((D, HID), jnp.float32)
        for replica in range(REPLICAS):
            input_grad, gate_part, up_part, down_part = expert_pass(
                tokens_in[replica, expert], grad_rows[replica, expert], combine_weights[replica, expert],
                live_counts[replica, expert], gate_weight, up_weight, down_weight)
            inputs_list.append(input_grad)
            gate_total = gate_total + lax.optimization_barrier(gate_part).astype(jnp.float32)
            up_total = up_total + lax.optimization_barrier(up_part).astype(jnp.float32)
            down_total = down_total + lax.optimization_barrier(down_part).astype(jnp.float32)
        return (jnp.stack(inputs_list), gate_total.astype(jnp.bfloat16), up_total.astype(jnp.bfloat16), down_total.astype(jnp.bfloat16))

    stacked, grad_gate, grad_up, grad_down = lax.map(per_expert, jnp.arange(NODES, dtype=jnp.int32))
    d_tokens = jnp.transpose(stacked, (1, 3, 2, 0, 4))
    return d_tokens, grad_gate, grad_up, grad_down
```

```python
import jax
import jax.numpy as jnp
from jax import lax
from jax.sharding import PartitionSpec as P


def on_device(tokens_in, grad_rows, combine_weights, live_counts, w_gate, w_up, w_down):
    slots, nodes, width = tokens_in.shape[2:]
    replicas, locals_ = lax.axis_size("dp"), lax.axis_size("local")
    replica, local, node = lax.axis_index("dp"), lax.axis_index("local"), lax.axis_index("node")
    keep = slots // locals_
    part = width // replicas
    rows = slots * nodes
    gate_weight, up_weight, down_weight = w_gate[0], w_up[0], w_down[0]
    tokens, grads = tokens_in[0, 0], grad_rows[0, 0]
    live = (lax.broadcasted_iota(jnp.int32, (slots, nodes), 0) < live_counts[0, 0][None, :]).astype(jnp.float32)
    factor = combine_weights[0, 0] * live

    def swap_local(value, bit):
        return lax.ppermute(value, "local", [(i, i ^ bit) for i in range(locals_)])

    def shift(value, axis, by):
        size = lax.axis_size(axis)
        return lax.ppermute(value, axis, [(i, (i + by) % size) for i in range(size)])

    bits = [1 << i for i in range(locals_.bit_length() - 1)]
    order = [0]
    for bit in reversed(bits):
        order = order + [d ^ bit for d in order]

    def gather_local(value):
        for bit in reversed(bits):
            value = jnp.concatenate((value, swap_local(value, bit)), axis=0)
        return value

    others = []
    for by in range(1, replicas):
        there = lax.rem(replica + by, replicas)
        start = (local * keep, 0, there * part)
        token_share = lax.dynamic_slice(tokens, start, (keep, nodes, part))
        grad_share = lax.dynamic_slice(grads, start, (keep, nodes, part))
        factor_share = lax.dynamic_slice(factor, (local * keep, 0), (keep, nodes))
        scaled_share = (grad_share.astype(jnp.float32) * factor_share[:, :, None]).astype(jnp.bfloat16)
        token_share = shift(token_share.reshape(keep * nodes, part), "dp", by)
        scaled_share = shift(scaled_share.reshape(keep * nodes, part), "dp", by)
        others.append((token_share, scaled_share))

    scaled = (grads.astype(jnp.float32) * factor[:, :, None]).astype(jnp.bfloat16).reshape(rows, width)
    tokens = tokens.reshape(rows, width)
    gate_pre = jnp.dot(tokens, gate_weight, preferred_element_type=jnp.float32)
    up_pre = jnp.dot(tokens, up_weight, preferred_element_type=jnp.float32)
    sigmoid_gate = jax.nn.sigmoid(gate_pre)
    activated = gate_pre * sigmoid_gate
    hidden = (activated * up_pre).astype(jnp.bfloat16)
    hidden_grad = jnp.dot(scaled, down_weight, preferred_element_type=jnp.float32)
    gate_grad = (hidden_grad * up_pre * sigmoid_gate * (1.0 + gate_pre * (1.0 - sigmoid_gate))).astype(jnp.bfloat16)
    up_grad = (hidden_grad * activated).astype(jnp.bfloat16)

    blocks = jnp.array(order) ^ local

    def reorder(value):
        return jnp.take(value.reshape(locals_, keep * nodes, -1), blocks, axis=0).reshape(rows, -1)

    sent = [[shift(reorder(v), "dp", by) for v in (gate_grad, up_grad, hidden)] for by in range(1, replicas)]

    place = local ^ jnp.arange(locals_)
    source = lax.rem(node + jnp.arange(nodes), nodes)
    index = ((place[:, None, None] * keep + jnp.arange(keep)[None, None, :]) * nodes + source[None, :, None]).reshape(-1)
    one_hot = (index[:, None] == jnp.arange(rows)[None, :]).astype(jnp.bfloat16)
    gate_moved = jnp.dot(one_hot, gate_grad, preferred_element_type=jnp.bfloat16)
    up_moved = jnp.dot(one_hot, up_grad, preferred_element_type=jnp.bfloat16)
    total = lax.dot_general(gate_moved, gate_weight, (((1,), (1,)), ((), ())), preferred_element_type=jnp.float32)
    total = total + lax.dot_general(up_moved, up_weight, (((1,), (1,)), ((), ())), preferred_element_type=jnp.float32)
    total = total.astype(jnp.bfloat16).reshape(locals_, nodes, keep, width)
    arrived = [None] * nodes
    for k in list(range(1, nodes)) + [0]:
        held = {d: total[d, k] for d in range(locals_)}
        for bit in bits:
            stay = sorted(d for d in held if not d & bit)
            came = swap_local(jnp.stack([held[d | bit] for d in stay]), bit)
            held = {d: (held[d].astype(jnp.float32) + came[i].astype(jnp.float32)).astype(jnp.bfloat16) for i, d in enumerate(stay)}
        arrived[k] = shift(held[0], "node", k) if k else held[0]
    stacked = jnp.stack(arrived)
    origin = lax.rem(node - jnp.arange(nodes) + nodes, nodes)
    d_tokens = jnp.take(stacked, origin, axis=0).transpose(1, 0, 2)[None, None]

    mine = lambda v: lax.dynamic_slice(v, (0, replica * part), (rows, part))
    token_parts, scaled_parts = [mine(tokens)], [mine(scaled)]
    gate_parts, up_parts, hidden_parts = [gate_grad], [up_grad], [hidden]
    for (token_share, scaled_share), (gg, ug, hd) in zip(others, sent):
        token_parts.append(gather_local(token_share))
        scaled_parts.append(gather_local(scaled_share))
        gate_parts.append(gg)
        up_parts.append(ug)
        hidden_parts.append(hd)

    def weight_grad(left, right):
        total = 0.0
        for a, b in zip(left, right):
            total = total + lax.dot_general(a, b, (((0,), (0,)), ((), ())), preferred_element_type=jnp.float32)
        return total.astype(jnp.bfloat16)[None]

    return (d_tokens, weight_grad(token_parts, gate_parts), weight_grad(token_parts, up_parts), weight_grad(scaled_parts, hidden_parts))


def solution(mesh):
    return jax.shard_map(
        on_device,
        mesh=mesh,
        in_specs=(
            P("dp", "node", None, None, None),
            P("dp", "node", None, None, None),
            P("dp", "node", None, None),
            P("dp", "node", None),
            P("node", None, "local"),
            P("node", None, "local"),
            P("node", None, "local"),
        ),
        out_specs=(
            P("dp", "node", "local", None, None),
            P("node", "dp", "local"),
            P("node", "dp", "local"),
            P("node", "dp", "local"),
        ),
        check_vma=False,
    )
```

```python
import functools

import jax
import jax.numpy as jnp
from jax import lax
from jax.experimental import pallas as pl
from jax.experimental.pallas import tpu as pltpu
from jax.sharding import PartitionSpec as P

F32, BF16 = jnp.float32, jnp.bfloat16
VMEM_LIMIT = 56 * 1024 * 1024


def dot(a, b, contract_a, contract_b):
    return lax.dot_general(a, b, (((contract_a,), (contract_b,)), ((), ())), preferred_element_type=F32)


def flat_rows(block):
    return block.reshape(block.shape[0] * block.shape[1], block.shape[2])


def log2(n):
    assert n & (n - 1) == 0
    return n.bit_length() - 1


def halving_order(size):
    order = [0]
    for i in reversed(range(log2(size))):
        order = order + [d ^ (1 << i) for d in order]
    return order


def bit_reverse(value, bits):
    out = jnp.zeros_like(value)
    for i in range(bits):
        out = out | (((value >> i) & 1) << (bits - 1 - i))
    return out


def forward_kernel(locals_, chunk, tok_hbm, grad_hbm, factor_ref, wg_hbm, wu_hbm, wd_hbm,
                   pair_hbm, hid_hbm, own_hbm, send_hbm,
                   tok, grad, wg, wu, wd, acc_g, acc_u, acc_h, pair, hid, total, in_sem, out_sem):
    slots, nodes, width = tok.shape
    rows = slots * nodes
    keep = slots // locals_
    steps = width // chunk
    me, node = lax.axis_index("local"), lax.axis_index("node")

    def fetch(i):
        cols = pl.ds(i * chunk, chunk)
        pairs = [(tok_hbm.at[:, :, cols], tok.at[:, :, cols]), (wg_hbm.at[cols], wg.at[cols]), (wu_hbm.at[cols], wu.at[cols]),
                 (grad_hbm.at[:, :, cols], grad.at[:, :, cols]), (wd_hbm.at[cols], wd.at[cols])]
        return [pltpu.make_async_copy(src, dst, in_sem.at[i, n]) for n, (src, dst) in enumerate(pairs)]

    for i in range(steps):
        for copy in fetch(i):
            copy.start()
    for i in range(steps):
        cols = pl.ds(i * chunk, chunk)
        copies = fetch(i)
        for copy in copies[:3]:
            copy.wait()
        t = flat_rows(tok[:, :, cols])
        gate = dot(t, wg[cols], 1, 0)
        up = dot(t, wu[cols], 1, 0)
        for copy in copies[3:]:
            copy.wait()
        scaled = (flat_rows(grad[:, :, cols].astype(F32)) * factor_ref[...]).astype(BF16)
        back = dot(scaled, wd[cols], 1, 0)
        if i:
            acc_g[...] += gate
            acc_u[...] += up
            acc_h[...] += back
        else:
            acc_g[...] = gate
            acc_u[...] = up
            acc_h[...] = back

    band = 64

    def activate(i, carry):
        at = pl.ds(pl.multiple_of(i * band, band), band)
        gate, up, back = acc_g[at], acc_u[at], acc_h[at]
        sig = jax.nn.sigmoid(gate)
        act = gate * sig
        hid[at] = (act * up).astype(BF16)
        pair[0, at] = (back * up * sig * (1.0 + gate * (1.0 - sig))).astype(BF16)
        pair[1, at] = (back * act).astype(BF16)
        return carry

    lax.fori_loop(0, rows // band, activate, 0)
    acts_out = [pltpu.make_async_copy(pair, pair_hbm, out_sem.at[0]), pltpu.make_async_copy(hid, hid_hbm, out_sem.at[1])]
    for copy in acts_out:
        copy.start()

    p = lax.broadcasted_iota(jnp.int32, (rows, rows), 0)
    j = p & (keep - 1)
    low = (p >> log2(keep)) & (locals_ // 2 - 1)
    k = (p >> log2(keep * locals_ // 2)) & (nodes - 1)
    high = p >> (log2(rows) - 1)
    place = bit_reverse(high * (locals_ // 2) + low, log2(locals_)) ^ me
    index = (place * keep + j) * nodes + ((node + k) & (nodes - 1))
    one_hot = jnp.where(index == lax.broadcasted_iota(jnp.int32, (rows, rows), 1), 1.0, 0.0).astype(BF16)
    gate_moved = dot(one_hot, pair[0], 1, 0).astype(BF16)
    up_moved = dot(one_hot, pair[1], 1, 0).astype(BF16)
    half = rows // 2

    def leave(i):
        cols = pl.ds(i * chunk, chunk)
        return [pltpu.make_async_copy(total.at[:half, cols], own_hbm.at[:, cols], out_sem.at[2 + 2 * i]),
                pltpu.make_async_copy(total.at[half:, cols], send_hbm.at[:, cols], out_sem.at[3 + 2 * i])]

    for i in range(steps):
        cols = pl.ds(i * chunk, chunk)
        total[:, cols] = (dot(gate_moved, wg[cols], 1, 1) + dot(up_moved, wu[cols], 1, 1)).astype(BF16)
        for copy in leave(i):
            copy.start()
    for copy in acts_out:
        copy.wait()
    for i in range(steps):
        for copy in leave(i):
            copy.wait()


def forward(locals_, tokens, grads, factor, gate_weight, up_weight, down_weight):
    slots, nodes, width = tokens.shape
    rows = slots * nodes
    hid_local = gate_weight.shape[1]
    chunk = 512
    steps = width // chunk
    hbm = pl.BlockSpec(memory_space=pl.ANY)
    weight = pltpu.VMEM(gate_weight.shape, BF16)
    acc = pltpu.VMEM((rows, hid_local), F32)
    return pl.pallas_call(
        functools.partial(forward_kernel, locals_, chunk),
        out_shape=[
            jax.ShapeDtypeStruct((2, rows, hid_local), BF16),
            jax.ShapeDtypeStruct((rows, hid_local), BF16),
            jax.ShapeDtypeStruct((rows // 2, width), BF16),
            jax.ShapeDtypeStruct((rows // 2, width), BF16),
        ],
        in_specs=[hbm, hbm, pl.BlockSpec(memory_space=pltpu.VMEM), hbm, hbm, hbm],
        out_specs=[hbm] * 4,
        scratch_shapes=[
            pltpu.VMEM(tokens.shape, BF16), pltpu.VMEM(tokens.shape, BF16), weight, weight, weight, acc, acc, acc,
            pltpu.VMEM((2, rows, hid_local), BF16), pltpu.VMEM((rows, hid_local), BF16), pltpu.VMEM((rows, width), BF16),
            pltpu.SemaphoreType.DMA((steps, 5)), pltpu.SemaphoreType.DMA((2 + 2 * steps,)),
        ],
        compiler_params=pltpu.CompilerParams(vmem_limit_bytes=VMEM_LIMIT),
        cost_estimate=pl.CostEstimate(flops=10 * rows * width * hid_local, bytes_accessed=18_000_000, transcendentals=0),
        name="forward",
    )(tokens, grads, factor, gate_weight, up_weight, down_weight)


def weight_kernel(order, count, scaled, *refs):
    rows_ref, factor_ref = refs[0], refs[1]
    shares = refs[2:2 + len(order)]
    own_refs = refs[2 + len(order):2 + len(order) + count]
    there_refs = refs[2 + len(order) + count:2 + len(order) + 2 * count]
    outs = refs[2 + len(order) + 2 * count:2 + len(order) + 3 * count]
    me = lax.axis_index("local")
    own = flat_rows(rows_ref[...])
    if scaled:
        own = (own.astype(F32) * factor_ref[...]).astype(BF16)
    left = jnp.concatenate([own] + [flat_rows(s[0]) for s in shares], axis=0)
    block = shares[0].shape[1] * shares[0].shape[2]
    for own_ref, there_ref, out in zip(own_refs, there_refs, outs):
        own_act = own_ref[...].reshape(own_ref.shape[-2:])
        there = there_ref.at[0] if len(there_ref.shape) == 3 else there_ref
        right = jnp.concatenate(
            [own_act] + [there[pl.ds(pl.multiple_of((me ^ d) * block, block), block), :] for d in order], axis=0)
        out[...] = dot(left, right, 0, 0).astype(BF16)


def weight_grads(order, scaled, replica, rows3, factor, shares, own_acts, there_acts, count):
    slots, nodes, width = rows3.shape
    part = shares[0].shape[-1]
    hid_local = own_acts.shape[-1]
    fb = 256
    per = part // fb
    which = 1 if scaled else 0
    rows = slots * nodes
    if count == 1:
        acts = [own_acts]
        theres = [there_acts]
        act_specs = [pl.BlockSpec((rows, hid_local), lambda i, r: (0, 0))]
    else:
        acts = [own_acts] * count
        theres = [there_acts] * count
        act_specs = [pl.BlockSpec((1, rows, hid_local), functools.partial(lambda n, i, r: (n, 0, 0), n)) for n in range(count)]
    out = pl.pallas_call(
        functools.partial(weight_kernel_prefetch, order, count, scaled),
        out_shape=[jax.ShapeDtypeStruct((part, hid_local), BF16)] * count,
        grid_spec=pltpu.PrefetchScalarGridSpec(
            num_scalar_prefetch=1,
            grid=(per,),
            in_specs=[pl.BlockSpec((slots, nodes, fb), lambda i, r: (0, 0, r[0] * per + i)),
                      pl.BlockSpec((rows, 1), lambda i, r: (0, 0))]
            + [pl.BlockSpec((1,) + shares[0].shape[1:3] + (fb,), lambda i, r: (which, 0, 0, i))] * len(shares)
            + act_specs + act_specs,
            out_specs=[pl.BlockSpec((fb, hid_local), lambda i, r: (i, 0))] * count,
        ),
        compiler_params=pltpu.CompilerParams(vmem_limit_bytes=VMEM_LIMIT),
        cost_estimate=pl.CostEstimate(flops=4 * rows * part * hid_local * count, bytes_accessed=4_000_000, transcendentals=0),
        name="weight_grads",
    )(replica, rows3, factor, *shares, *acts, *theres)
    return out


def weight_kernel_prefetch(order, count, scaled, replica_ref, *refs):
    weight_kernel(order, count, scaled, *refs)


def collect_kernel(*refs):
    *arrived, kept, came, out = refs
    keep, nodes, width = out.shape
    node = lax.axis_index("node")
    last = (kept[...].astype(F32) + came[...].astype(F32)).astype(BF16)
    stacked = jnp.concatenate([last] + [a[...] for a in arrived], axis=0)
    rows = keep * nodes
    p = lax.broadcasted_iota(jnp.int32, (rows, rows), 0)
    source = ((node - (p & (nodes - 1))) & (nodes - 1)) * keep + (p >> log2(nodes))
    one_hot = jnp.where(source == lax.broadcasted_iota(jnp.int32, (rows, rows), 1), 1.0, 0.0).astype(BF16)
    out[...] = dot(one_hot, stacked, 1, 0).astype(BF16).reshape(out.shape)


def on_device(tokens_in, grad_rows, combine_weights, live_counts, w_gate, w_up, w_down):
    slots, nodes, width = tokens_in.shape[2:]
    replicas, locals_ = lax.axis_size("dp"), lax.axis_size("local")
    assert replicas == 2
    replica, local = lax.axis_index("dp"), lax.axis_index("local")
    keep = slots // locals_
    part = width // replicas
    rows = slots * nodes
    gate_weight, up_weight, down_weight = w_gate[0], w_up[0], w_down[0]
    tokens, grads = tokens_in[0, 0], grad_rows[0, 0]
    live = (lax.broadcasted_iota(jnp.int32, (slots, nodes), 0) < live_counts[0, 0][None, :]).astype(F32)
    factor = combine_weights[0, 0] * live
    column = factor.reshape(rows, 1)
    order = halving_order(locals_)
    bits = [1 << i for i in range(log2(locals_))]

    def swap_local(value, bit):
        return lax.ppermute(value, "local", [(i, i ^ bit) for i in range(locals_)])

    def swap_dp(value):
        return lax.ppermute(value, "dp", [(0, 1), (1, 0)])

    start = (local * keep, 0, (1 - replica) * part)
    token_share = lax.dynamic_slice(tokens, start, (keep, nodes, part))
    grad_share = lax.dynamic_slice(grads, start, (keep, nodes, part))
    factor_share = lax.dynamic_slice(factor, (local * keep, 0), (keep, nodes))
    scaled_share = (grad_share.astype(F32) * factor_share[:, :, None]).astype(BF16)
    shares = [swap_dp(jnp.stack((token_share, scaled_share)))]
    for bit in reversed(bits):
        shares = shares + [swap_local(v, bit) for v in shares]

    pair, hidden, own, send = forward(locals_, tokens, grads, column, gate_weight, up_weight, down_weight)
    pair_there = swap_dp(pair)
    hidden_there = swap_dp(hidden)

    came = swap_local(send, bits[0])
    size = locals_ // 2
    own = own.reshape(nodes, size * keep, width)
    came = came.reshape(nodes, size * keep, width)
    arrived = [None] * nodes
    for k in list(range(1, nodes)) + [0]:
        mine, other = own[k], came[k]
        n = size
        for bit in bits[1:]:
            total = (mine.astype(F32) + other.astype(F32)).astype(BF16)
            n //= 2
            mine = total[: n * keep]
            other = swap_local(total[n * keep :], bit)
        if k:
            arrived[k] = lax.ppermute((mine.astype(F32) + other.astype(F32)).astype(BF16), "node",
                                      [(i, (i + k) % nodes) for i in range(nodes)])
        else:
            arrived[0] = (mine, other)
    d_tokens = pl.pallas_call(
        collect_kernel,
        out_shape=jax.ShapeDtypeStruct((keep, nodes, width), BF16),
        compiler_params=pltpu.CompilerParams(vmem_limit_bytes=VMEM_LIMIT),
        name="collect",
    )(*arrived[1:], *arrived[0])

    where = replica.reshape(1).astype(jnp.int32)
    grad_gate, grad_up = weight_grads(order, False, where, tokens, column, shares, pair, pair_there, 2)
    (grad_down,) = weight_grads(order, True, where, grads, column, shares, hidden, hidden_there, 1)
    return d_tokens[None, None], grad_gate[None], grad_up[None], grad_down[None]


def solution(mesh):
    return jax.shard_map(
        on_device,
        mesh=mesh,
        in_specs=(
            P("dp", "node", None, None, None),
            P("dp", "node", None, None, None),
            P("dp", "node", None, None),
            P("dp", "node", None),
            P("node", None, "local"),
            P("node", None, "local"),
            P("node", None, "local"),
        ),
        out_specs=(
            P("dp", "node", "local", None, None),
            P("node", "dp", "local"),
            P("node", "dp", "local"),
            P("node", "dp", "local"),
        ),
        check_vma=False,
    )
```

```python
import functools

import jax
import jax.numpy as jnp
from jax import lax
from jax.experimental import pallas as pl
from jax.experimental.pallas import tpu as pltpu
from jax.sharding import PartitionSpec as P

F32, BF16 = jnp.float32, jnp.bfloat16
VMEM_LIMIT = 24 * 1024 * 1024


def dot(a, b, contract_a, contract_b):
    return lax.dot_general(a, b, (((contract_a,), (contract_b,)), ((), ())), preferred_element_type=F32)


def flat_rows(block):
    return block.reshape(block.shape[0] * block.shape[1], block.shape[2])


def log2(n):
    assert n & (n - 1) == 0
    return n.bit_length() - 1


def halving_order(size):
    order = [0]
    for i in reversed(range(log2(size))):
        order = order + [d ^ (1 << i) for d in order]
    return order


def bit_reverse(value, bits):
    out = jnp.zeros_like(value)
    for i in range(bits):
        out = out | (((value >> i) & 1) << (bits - 1 - i))
    return out


def shift_order(nodes):
    return sorted(range(1, nodes), key=lambda k: (-min(k, nodes - k), k)) + [0]


def column(weights, counts, first, out_rows):
    slots, nodes = weights.shape
    slot = first + lax.broadcasted_iota(jnp.int32, (slots, nodes), 0)
    factor = weights * jnp.where(slot < counts, 1.0, 0.0)
    spread = jnp.broadcast_to(factor[:, None, :], (slots, nodes, nodes)).reshape(out_rows, nodes)
    row = lax.broadcasted_iota(jnp.int32, (out_rows, nodes), 0)
    lane = lax.broadcasted_iota(jnp.int32, (out_rows, nodes), 1)
    return jnp.sum(jnp.where((row & (nodes - 1)) == lane, spread, 0.0), axis=1, keepdims=True)


def share_kernel(locals_, tok_hbm, grad_hbm, weights_ref, counts_ref, out, tok, grad, sem):
    keep, nodes, part = tok.shape
    me, other = lax.axis_index("local"), 1 - lax.axis_index("dp")
    slots = pl.ds(me * keep, keep)
    cols = pl.ds(pl.multiple_of(other * part, 128), part)
    copies = [pltpu.make_async_copy(tok_hbm.at[slots, :, cols], tok, sem.at[0]),
              pltpu.make_async_copy(grad_hbm.at[slots, :, cols], grad, sem.at[1])]
    for copy in copies:
        copy.start()
    factor = column(weights_ref[slots], counts_ref[...], me * keep, keep * nodes)
    copies[0].wait()
    out[0] = flat_rows(tok[...])
    copies[1].wait()
    out[1] = (flat_rows(grad[...].astype(F32)) * factor).astype(BF16)


def share(locals_, tokens, grads, weights, counts):
    slots, nodes, width = tokens.shape
    keep, part = slots // locals_, width // 2
    vmem, hbm = pl.BlockSpec(memory_space=pltpu.VMEM), pl.BlockSpec(memory_space=pltpu.HBM)
    return pl.pallas_call(
        functools.partial(share_kernel, locals_),
        out_shape=jax.ShapeDtypeStruct((2, keep * nodes, part), BF16),
        in_specs=[hbm, hbm, vmem, vmem],
        out_specs=vmem,
        scratch_shapes=[pltpu.VMEM((keep, nodes, part), BF16)] * 2 + [pltpu.SemaphoreType.DMA((2,))],
        compiler_params=pltpu.CompilerParams(vmem_limit_bytes=VMEM_LIMIT),
        name="share",
    )(tokens, grads, weights, counts)


def forward_kernel(locals_, tok, grad, weights_ref, counts_ref, wg, wu, wd, pair, hid, own_a, own_b, send_a, send_b,
                   acc_g, acc_u, acc_h, moved):
    slots, nodes, width = tok.shape
    rows = slots * nodes
    keep = slots // locals_
    chunk = 512
    steps = width // chunk
    me, node = lax.axis_index("local"), lax.axis_index("node")
    factor = column(weights_ref[...], counts_ref[...], 0, rows)

    for i in range(steps):
        cols = pl.ds(i * chunk, chunk)
        t = flat_rows(tok[:, :, cols])
        gate = dot(t, wg[cols], 1, 0)
        up = dot(t, wu[cols], 1, 0)
        scaled = (flat_rows(grad[:, :, cols].astype(F32)) * factor).astype(BF16)
        back = dot(scaled, wd[cols], 1, 0)
        if i:
            acc_g[...] += gate
            acc_u[...] += up
            acc_h[...] += back
        else:
            acc_g[...] = gate
            acc_u[...] = up
            acc_h[...] = back

    band = 64

    def activate(i, carry):
        at = pl.ds(pl.multiple_of(i * band, band), band)
        gate, up, back = acc_g[at], acc_u[at], acc_h[at]
        sig = jax.nn.sigmoid(gate)
        act = gate * sig
        hid[at] = (act * up).astype(BF16)
        pair[0, at] = (back * up * sig * (1.0 + gate * (1.0 - sig))).astype(BF16)
        pair[1, at] = (back * act).astype(BF16)
        return carry

    lax.fori_loop(0, rows // band, activate, 0)

    per = nodes // 2
    p = lax.broadcasted_iota(jnp.int32, (rows, 1), 0)
    j = p & (keep - 1)
    at = log2(keep)
    quick = (p >> at) & (per - 1)
    at += log2(per)
    low = (p >> at) & (locals_ // 2 - 1)
    at += log2(locals_ // 2)
    group = (p >> at) & 1
    high = p >> (at + 1)
    place = bit_reverse(high * (locals_ // 2) + low, log2(locals_)) ^ me
    hop = jnp.zeros_like(p)
    for n, k in enumerate(shift_order(nodes)):
        hop = jnp.where(group * per + quick == n, k, hop)
    index = (place * keep + j) * nodes + ((node + hop) & (nodes - 1))
    one_hot = jnp.where(index == lax.broadcasted_iota(jnp.int32, (rows, rows), 1), 1.0, 0.0).astype(BF16)
    moved[0] = dot(one_hot, pair[0], 1, 0).astype(BF16)
    moved[1] = dot(one_hot, pair[1], 1, 0).astype(BF16)
    quarter = rows // 4
    for i in range(steps):
        cols = pl.ds(i * chunk, chunk)
        total = (dot(moved[0], wg[cols], 1, 1) + dot(moved[1], wu[cols], 1, 1)).astype(BF16)
        for n, out in enumerate((own_a, own_b, send_a, send_b)):
            out[:, cols] = total[n * quarter:(n + 1) * quarter]


def forward(locals_, tokens, grads, weights, counts, gate_weight, up_weight, down_weight):
    slots, nodes, width = tokens.shape
    rows = slots * nodes
    hid_local = gate_weight.shape[1]
    vmem = pl.BlockSpec(memory_space=pltpu.VMEM)
    acc = pltpu.VMEM((rows, hid_local), F32)
    return pl.pallas_call(
        functools.partial(forward_kernel, locals_),
        out_shape=[jax.ShapeDtypeStruct((2, rows, hid_local), BF16), jax.ShapeDtypeStruct((rows, hid_local), BF16)]
        + [jax.ShapeDtypeStruct((rows // 4, width), BF16)] * 4,
        in_specs=[vmem] * 7,
        out_specs=[vmem] * 6,
        scratch_shapes=[acc, acc, acc, pltpu.VMEM((2, rows, hid_local), BF16)],
        compiler_params=pltpu.CompilerParams(vmem_limit_bytes=VMEM_LIMIT),
        cost_estimate=pl.CostEstimate(flops=10 * rows * width * hid_local, bytes_accessed=18_000_000, transcendentals=0),
        name="forward",
    )(tokens, grads, weights, counts, gate_weight, up_weight, down_weight)


def weight_kernel(order, count, *refs):
    rows_ref, weights_ref, counts_ref = refs[:3]
    shares = refs[3:3 + len(order)]
    own_ref, there_ref = refs[3 + len(order):5 + len(order)]
    outs = refs[5 + len(order):5 + len(order) + count]
    left, right, bufs, sem = refs[5 + len(order) + count:]
    slots, nodes, width = rows_ref.shape
    rows = slots * nodes
    part, hid_local = outs[0].shape
    me, replica = lax.axis_index("local"), lax.axis_index("dp")
    block = rows // len(order)
    which = 0 if count == 2 else 1
    factor = None if count == 2 else column(weights_ref[...], counts_ref[...], 0, rows)
    for n in range(count):
        right[n, :rows] = own_ref[n]
        for b, d in enumerate(order):
            right[n, rows + b * block:rows + (b + 1) * block] = there_ref[n, pl.ds(pl.multiple_of((me ^ d) * block, block), block)]
    chunk = 896
    copies = []
    for i in range(part // chunk):
        cols = pl.ds(i * chunk, chunk)
        own = rows_ref[:, :, pl.ds(pl.multiple_of(replica * part + i * chunk, 128), chunk)]
        left[:rows] = flat_rows(own) if count == 2 else (flat_rows(own.astype(F32)) * factor).astype(BF16)
        for b, ref in enumerate(shares):
            left[rows + b * block:rows + (b + 1) * block] = ref[which, :, cols]
        for n, out in enumerate(outs):
            bufs[n, cols] = dot(left[...], right[n], 0, 0).astype(BF16)
            copies.append(pltpu.make_async_copy(bufs.at[n, cols], out.at[cols], sem.at[i, n]))
            copies[-1].start()
    for copy in copies:
        copy.wait()


def weight_grads(order, rows3, weights, counts, shares, own_acts, there_acts):
    slots, nodes, width = rows3.shape
    part = shares[0].shape[-1]
    count, rows, hid_local = own_acts.shape
    vmem = pl.BlockSpec(memory_space=pltpu.VMEM)
    return pl.pallas_call(
        functools.partial(weight_kernel, order, count),
        out_shape=[jax.ShapeDtypeStruct((part, hid_local), BF16)] * count,
        in_specs=[vmem] * (5 + len(shares)),
        out_specs=[pl.BlockSpec(memory_space=pltpu.HBM)] * count,
        scratch_shapes=[pltpu.VMEM((2 * rows, 896), BF16), pltpu.VMEM((count, 2 * rows, hid_local), BF16),
                        pltpu.VMEM((count, part, hid_local), BF16), pltpu.SemaphoreType.DMA((part // 896, count))],
        compiler_params=pltpu.CompilerParams(vmem_limit_bytes=VMEM_LIMIT),
        cost_estimate=pl.CostEstimate(flops=4 * rows * part * hid_local * count, bytes_accessed=4_000_000, transcendentals=0),
        name="weight_grads",
    )(rows3, weights, counts, *shares, own_acts, there_acts)


def collect_kernel(*refs):
    *arrived, kept, came, out = refs
    keep, nodes, width = out.shape
    node = lax.axis_index("node")
    last = (kept[...].astype(F32) + came[...].astype(F32)).astype(BF16)
    stacked = jnp.concatenate([last] + [a[...] for a in arrived], axis=0)
    rows = keep * nodes
    p = lax.broadcasted_iota(jnp.int32, (rows, rows), 0)
    source = ((node - (p & (nodes - 1))) & (nodes - 1)) * keep + (p >> log2(nodes))
    one_hot = jnp.where(source == lax.broadcasted_iota(jnp.int32, (rows, rows), 1), 1.0, 0.0).astype(BF16)
    out[...] = dot(one_hot, stacked, 1, 0).astype(BF16).reshape(out.shape)


def add(a, b):
    return (a.astype(F32) + b.astype(F32)).astype(BF16)


def on_device(tokens_in, grad_rows, combine_weights, live_counts, w_gate, w_up, w_down):
    slots, nodes, width = tokens_in.shape[2:]
    replicas, locals_ = lax.axis_size("dp"), lax.axis_size("local")
    assert replicas == 2
    keep = slots // locals_
    tokens, grads, weights, counts = tokens_in[0, 0], grad_rows[0, 0], combine_weights[0, 0], live_counts[0]
    order = halving_order(locals_)
    bits = [1 << i for i in range(log2(locals_))]

    def swap_local(value, bit):
        return lax.ppermute(value, "local", [(i, i ^ bit) for i in range(locals_)])

    def swap_dp(value):
        return lax.ppermute(value, "dp", [(0, 1), (1, 0)])

    def gather_shares(value):
        out = [value]
        for bit in reversed(bits):
            out = out + [swap_local(v, bit) for v in out]
        return out

    first = swap_dp(share(locals_, tokens, grads, weights, counts))
    pair, hidden, own_a, own_b, send_a, send_b = forward(locals_, tokens, grads, weights, counts, w_gate[0], w_up[0], w_down[0])
    pair_there = swap_dp(pair)
    hidden_there = swap_dp(hidden)
    send_a, send_b, first = lax.optimization_barrier((send_a, send_b, first))
    shares = gather_shares(first)

    per = nodes // 2
    hops = shift_order(nodes)
    arrived = [None] * nodes
    held = [(own_a, swap_local(send_a, bits[0])), (own_b, swap_local(send_b, bits[0]))]
    for bit in bits[1:]:
        for g, (mine, other) in enumerate(held):
            half = mine.shape[0] // 2
            held[g] = (add(mine[:half], other[:half]), swap_local(add(mine[half:], other[half:]), bit))
    for n, k in enumerate(hops):
        mine, other = (v[n % per * keep:(n % per + 1) * keep] for v in held[n // per])
        if k:
            arrived[k] = lax.ppermute(add(mine, other), "node", [(i, (i + k) % nodes) for i in range(nodes)])
        else:
            arrived[0] = (mine, other)
    d_tokens = pl.pallas_call(
        collect_kernel,
        out_shape=jax.ShapeDtypeStruct((keep, nodes, width), BF16),
        in_specs=[pl.BlockSpec(memory_space=pltpu.VMEM)] * (nodes + 1),
        out_specs=pl.BlockSpec(memory_space=pltpu.VMEM),
        compiler_params=pltpu.CompilerParams(vmem_limit_bytes=VMEM_LIMIT),
        name="collect",
    )(*arrived[1:], *arrived[0])

    grad_gate, grad_up = weight_grads(order, tokens, weights, counts, shares, pair, pair_there)
    (grad_down,) = weight_grads(order, grads, weights, counts, shares, hidden[None], hidden_there[None])
    return d_tokens[None, None], grad_gate[None], grad_up[None], grad_down[None]


def solution(mesh):
    return jax.shard_map(
        on_device,
        mesh=mesh,
        in_specs=(
            P("dp", "node", None, None, None),
            P("dp", "node", None, None, None),
            P("dp", "node", None, None),
            P("dp", "node", None),
            P("node", None, "local"),
            P("node", None, "local"),
            P("node", None, "local"),
        ),
        out_specs=(
            P("dp", "node", "local", None, None),
            P("node", "dp", "local"),
            P("node", "dp", "local"),
            P("node", "dp", "local"),
        ),
        check_vma=False,
    )
```

```python
import functools

import jax
import jax.numpy as jnp
from jax import lax
from jax.experimental import pallas as pl
from jax.experimental.pallas import tpu as pltpu
from jax.sharding import PartitionSpec as P

F32, BF16 = jnp.float32, jnp.bfloat16
MIB = 1024 * 1024
VMEM_LIMIT = 24 * MIB
VMEM = 58 * MIB


def dot(a, b, contract_a, contract_b):
    return lax.dot_general(a, b, (((contract_a,), (contract_b,)), ((), ())), preferred_element_type=F32)


def flat_rows(block):
    return block.reshape(block.shape[0] * block.shape[1], block.shape[2])


def log2(n):
    assert n & (n - 1) == 0
    return n.bit_length() - 1


def halving_order(size):
    order = [0]
    for i in reversed(range(log2(size))):
        order = order + [d ^ (1 << i) for d in order]
    return order


def bit_reverse(value, bits):
    out = jnp.zeros_like(value)
    for i in range(bits):
        out = out | (((value >> i) & 1) << (bits - 1 - i))
    return out


def shift_order(nodes):
    return sorted(range(1, nodes), key=lambda k: (-min(k, nodes - k), k)) + [0]


def column(weights, counts, first, out_rows):
    weights = weights.T
    slots, nodes = weights.shape
    slot = first + lax.broadcasted_iota(jnp.int32, (slots, nodes), 0)
    factor = weights * jnp.where(slot < counts, 1.0, 0.0)
    spread = jnp.broadcast_to(factor[:, None, :], (slots, nodes, nodes)).reshape(out_rows, nodes)
    row = lax.broadcasted_iota(jnp.int32, (out_rows, nodes), 0)
    lane = lax.broadcasted_iota(jnp.int32, (out_rows, nodes), 1)
    return jnp.sum(jnp.where((row & (nodes - 1)) == lane, spread, 0.0), axis=1, keepdims=True)


def pick_slots(weights, first, keep):
    out = weights[:, :keep]
    for at in range(keep, weights.shape[1], keep):
        out = jnp.where(first == at, weights[:, at:at + keep], out)
    return out


def share_kernel(blocks, tok_hbm, grad_hbm, weights_hbm, counts_hbm, out, tok, grad, weights, counts, sem):
    keep, nodes, part = tok.shape
    me, other = lax.axis_index("local"), 1 - lax.axis_index("dp")
    cols = pl.ds(pl.multiple_of(other * part, 128), part)
    firsts = [(me ^ d) * keep for d in blocks]
    copies = [pltpu.make_async_copy(grad_hbm.at[pl.ds(first, keep), :, cols], grad.at[b], sem.at[b]) for b, first in enumerate(firsts)]
    copies.append(pltpu.make_async_copy(tok_hbm.at[pl.ds(firsts[0], keep), :, cols], tok, sem.at[len(blocks)]))
    small = [pltpu.make_async_copy(weights_hbm, weights, sem.at[len(blocks) + 1]),
             pltpu.make_async_copy(counts_hbm, counts, sem.at[len(blocks) + 2])]
    for copy in small + copies:
        copy.start()
    rows = keep * nodes
    for copy in small:
        copy.wait()
    for b, first in enumerate(firsts):
        factor = column(pick_slots(weights[...], first, keep), counts[...], first, rows)
        copies[b].wait()
        out[b * rows:(b + 1) * rows] = (flat_rows(grad[b].astype(F32)) * factor).astype(BF16)
    copies[-1].wait()
    out[len(blocks) * rows:] = flat_rows(tok[...])


def share(order, tokens, grads, weights, counts):
    slots, nodes, width = tokens.shape
    keep, part = slots // len(order), width // 2
    blocks = order[:1]
    vmem, hbm = pl.BlockSpec(memory_space=pltpu.VMEM), pl.BlockSpec(memory_space=pltpu.HBM)
    return pl.pallas_call(
        functools.partial(share_kernel, blocks),
        out_shape=jax.ShapeDtypeStruct(((len(blocks) + 1) * keep * nodes, part), BF16),
        in_specs=[hbm] * 4,
        out_specs=vmem,
        scratch_shapes=[pltpu.VMEM((keep, nodes, part), BF16), pltpu.VMEM((len(blocks), keep, nodes, part), BF16),
                        pltpu.VMEM(weights.shape, F32), pltpu.VMEM(counts.shape, jnp.int32),
                        pltpu.SemaphoreType.DMA((len(blocks) + 3,))],
        compiler_params=pltpu.CompilerParams(vmem_limit_bytes=VMEM),
        name="share",
    )(tokens, grads, weights, counts)


def forward_kernel(locals_, chunk, tok_hbm, grad_hbm, weights_hbm, counts_hbm, wg_hbm, wu_hbm, wd_hbm,
                   acts, own_a, own_b, send_a, send_b,
                   tok, grad, weights, counts, wgu, wd, acc, acc_h, moved, sem):
    slots, nodes, width = tok.shape
    rows = slots * nodes
    keep = slots // locals_
    steps = width // chunk
    hid_local = wd.shape[1]
    me, node = lax.axis_index("local"), lax.axis_index("node")

    def fetch(i):
        cols = pl.ds(i * chunk, chunk)
        ends = [(tok_hbm.at[:, :, cols], tok.at[:, :, cols]), (wg_hbm.at[cols], wgu.at[cols, :hid_local]),
                (wu_hbm.at[cols], wgu.at[cols, hid_local:]), (grad_hbm.at[:, :, cols], grad.at[:, :, cols]), (wd_hbm.at[cols], wd.at[cols])]
        return [pltpu.make_async_copy(src, dst, sem.at[i, n]) for n, (src, dst) in enumerate(ends)]

    small = [pltpu.make_async_copy(weights_hbm, weights, sem.at[steps, 0]), pltpu.make_async_copy(counts_hbm, counts, sem.at[steps, 1])]
    copies = [fetch(i) for i in range(steps)]
    for group in [small] + copies:
        for copy in group:
            copy.start()
    for copy in small:
        copy.wait()
    factor = column(weights[...], counts[...], 0, rows)
    for i in range(steps):
        cols = pl.ds(i * chunk, chunk)
        for copy in copies[i][:3]:
            copy.wait()
        both = dot(flat_rows(tok[:, :, cols]), wgu[cols], 1, 0)
        for copy in copies[i][3:]:
            copy.wait()
        scaled = (flat_rows(grad[:, :, cols].astype(F32)) * factor).astype(BF16)
        back = dot(scaled, wd[cols], 1, 0)
        if i:
            acc[...] += both
            acc_h[...] += back
        else:
            acc[...] = both
            acc_h[...] = back

    band = 64

    def activate(i, carry):
        at = pl.ds(pl.multiple_of(i * band, band), band)
        gate, up, back = acc[at, :hid_local], acc[at, hid_local:], acc_h[at]
        sig = jax.nn.sigmoid(gate)
        act = gate * sig
        acts[2, at] = (act * up).astype(BF16)
        acts[0, at] = (back * up * sig * (1.0 + gate * (1.0 - sig))).astype(BF16)
        acts[1, at] = (back * act).astype(BF16)
        return carry

    lax.fori_loop(0, rows // band, activate, 0)

    per = nodes // 2
    p = lax.broadcasted_iota(jnp.int32, (rows, 1), 0)
    j = p & (keep - 1)
    at = log2(keep)
    quick = (p >> at) & (per - 1)
    at += log2(per)
    low = (p >> at) & (locals_ // 2 - 1)
    at += log2(locals_ // 2)
    group = (p >> at) & 1
    high = p >> (at + 1)
    place = bit_reverse(high * (locals_ // 2) + low, log2(locals_)) ^ me
    hop = jnp.zeros_like(p)
    for n, k in enumerate(shift_order(nodes)):
        hop = jnp.where(group * per + quick == n, k, hop)
    index = (place * keep + j) * nodes + ((node + hop) & (nodes - 1))
    one_hot = jnp.where(index == lax.broadcasted_iota(jnp.int32, (rows, rows), 1), 1.0, 0.0).astype(BF16)
    moved[:, :hid_local] = dot(one_hot, acts[0], 1, 0).astype(BF16)
    moved[:, hid_local:] = dot(one_hot, acts[1], 1, 0).astype(BF16)
    quarter = rows // 4
    for i in range(steps):
        cols = pl.ds(i * chunk, chunk)
        total = dot(moved[...], wgu[cols], 1, 1).astype(BF16)
        for n, out in enumerate((own_a, own_b, send_a, send_b)):
            out[:, cols] = total[n * quarter:(n + 1) * quarter]


def forward(locals_, tokens, grads, weights, counts, gate_weight, up_weight, down_weight):
    slots, nodes, width = tokens.shape
    rows = slots * nodes
    hid_local = gate_weight.shape[1]
    vmem, hbm = pl.BlockSpec(memory_space=pltpu.VMEM), pl.BlockSpec(memory_space=pltpu.HBM)
    chunk = 512
    outside = 2 * (3 * rows * hid_local + rows * width + tokens.size // 2)
    return pl.pallas_call(
        functools.partial(forward_kernel, locals_, chunk),
        out_shape=[jax.ShapeDtypeStruct((3, rows, hid_local), BF16)] + [jax.ShapeDtypeStruct((rows // 4, width), BF16)] * 4,
        in_specs=[hbm] * 7,
        out_specs=[vmem] * 5,
        scratch_shapes=[
            pltpu.VMEM(tokens.shape, BF16), pltpu.VMEM(tokens.shape, BF16), pltpu.VMEM(weights.shape, F32),
            pltpu.VMEM(counts.shape, jnp.int32), pltpu.VMEM((width, 2 * hid_local), BF16), pltpu.VMEM((width, hid_local), BF16),
            pltpu.VMEM((rows, 2 * hid_local), F32), pltpu.VMEM((rows, hid_local), F32), pltpu.VMEM((rows, 2 * hid_local), BF16),
            pltpu.SemaphoreType.DMA((width // chunk + 1, 5))],
        compiler_params=pltpu.CompilerParams(vmem_limit_bytes=VMEM - outside),
        cost_estimate=pl.CostEstimate(flops=10 * rows * width * hid_local, bytes_accessed=18_000_000, transcendentals=0),
        name="forward",
    )(tokens, grads, weights, counts, gate_weight, up_weight, down_weight)


def weight_kernel(order, pieces, acts_at, scaled, *refs):
    count = len(acts_at)
    rows_ref, weights_ref, counts_ref = refs[:3]
    shares = refs[3:3 + len(pieces)]
    own_ref, there_ref = refs[3 + len(pieces):5 + len(pieces)]
    outs = refs[5 + len(pieces):5 + len(pieces) + count]
    left, right, bufs, sem = refs[5 + len(pieces) + count:]
    slots, nodes, width = rows_ref.shape
    rows = slots * nodes
    part, hid_local = outs[0].shape
    me, replica = lax.axis_index("local"), lax.axis_index("dp")
    block = rows // len(order)
    factor = column(weights_ref[...], counts_ref[...], 0, rows) if scaled else None
    for n, a in enumerate(acts_at):
        right[n, :rows] = own_ref[a]
        for b, d in enumerate(order):
            right[n, rows + b * block:rows + (b + 1) * block] = there_ref[a, pl.ds(pl.multiple_of((me ^ d) * block, block), block)]
    chunk = left.shape[1]
    copies = []
    for i in range(part // chunk):
        cols = pl.ds(i * chunk, chunk)
        own = rows_ref[:, :, pl.ds(pl.multiple_of(replica * part + i * chunk, 128), chunk)]
        left[:rows] = (flat_rows(own.astype(F32)) * factor).astype(BF16) if scaled else flat_rows(own)
        at = rows
        for ref, (first, size) in zip(shares, pieces):
            left[at:at + size] = ref[first:first + size, cols]
            at += size
        for n, out in enumerate(outs):
            bufs[n, cols] = dot(left[...], right[n], 0, 0).astype(BF16)
            copies.append(pltpu.make_async_copy(bufs.at[n, cols], out.at[cols], sem.at[i, n]))
            copies[-1].start()
    for copy in copies:
        copy.wait()


def weight_grads(order, rows3, weights, counts, shares, pieces, own_acts, there_acts, acts_at, scaled):
    slots, nodes, width = rows3.shape
    part = shares[0].shape[-1]
    rows, hid_local = own_acts.shape[1:]
    count = len(acts_at)
    chunk = 896
    vmem = pl.BlockSpec(memory_space=pltpu.VMEM)
    return pl.pallas_call(
        functools.partial(weight_kernel, order, pieces, acts_at, scaled),
        out_shape=[jax.ShapeDtypeStruct((part, hid_local), BF16)] * count,
        in_specs=[vmem] * (5 + len(shares)),
        out_specs=[pl.BlockSpec(memory_space=pltpu.HBM)] * count,
        scratch_shapes=[pltpu.VMEM((2 * rows, chunk), BF16), pltpu.VMEM((count, 2 * rows, hid_local), BF16),
                        pltpu.VMEM((count, part, hid_local), BF16), pltpu.SemaphoreType.DMA((part // chunk, count))],
        compiler_params=pltpu.CompilerParams(vmem_limit_bytes=VMEM_LIMIT),
        cost_estimate=pl.CostEstimate(flops=4 * rows * part * hid_local * count, bytes_accessed=4_000_000, transcendentals=0),
        name="weight_grads",
    )(rows3, weights, counts, *shares, own_acts, there_acts)


def collect_kernel(*refs):
    *arrived, kept, came, out = refs
    keep, nodes, width = out.shape
    node = lax.axis_index("node")
    last = (kept[...].astype(F32) + came[...].astype(F32)).astype(BF16)
    stacked = jnp.concatenate([last] + [a[...] for a in arrived], axis=0)
    rows = keep * nodes
    p = lax.broadcasted_iota(jnp.int32, (rows, rows), 0)
    source = ((node - (p & (nodes - 1))) & (nodes - 1)) * keep + (p >> log2(nodes))
    one_hot = jnp.where(source == lax.broadcasted_iota(jnp.int32, (rows, rows), 1), 1.0, 0.0).astype(BF16)
    out[...] = dot(one_hot, stacked, 1, 0).astype(BF16).reshape(out.shape)


def after(value, other):
    return lax.optimization_barrier((value, other))[0]


def add(a, b):
    return (a.astype(F32) + b.astype(F32)).astype(BF16)


def on_device(tokens_in, grad_rows, combine_weights, live_counts, w_gate, w_up, w_down):
    slots, nodes, width = tokens_in.shape[2:]
    replicas, locals_ = lax.axis_size("dp"), lax.axis_size("local")
    assert replicas == 2
    keep = slots // locals_
    tokens, grads, weights, counts = tokens_in[0, 0], grad_rows[0, 0], combine_weights[0, 0].T, live_counts[0]
    order = halving_order(locals_)
    bits = [1 << i for i in range(log2(locals_))]

    def swap_local(value, bit):
        return lax.ppermute(value, "local", [(i, i ^ bit) for i in range(locals_)])

    def swap_dp(value):
        return lax.ppermute(value, "dp", [(0, 1), (1, 0)])

    rows = slots * nodes
    block = rows // locals_
    first, weights = lax.optimization_barrier((share(order, tokens, grads, weights, counts), weights))
    first = swap_dp(first)
    acts, own_a, own_b, send_a, send_b = forward(locals_, tokens, grads, weights, counts, w_gate[0], w_up[0], w_down[0])
    there = swap_dp(acts)

    per = nodes // 2
    hops = shift_order(nodes)
    arrived = [None] * nodes
    send_a, send_b = after(send_a, first), after(send_b, first)
    held = [(own_a, swap_local(send_a, bits[0])), (own_b, swap_local(send_b, bits[0]))]
    for bit in bits[1:]:
        for g, (mine, other) in enumerate(held):
            half = mine.shape[0] // 2
            held[g] = (add(mine[:half], other[:half]), swap_local(add(mine[half:], other[half:]), bit))
    first = after(first, held[0][1])
    shares = [first]
    for bit in reversed(bits[1:]):
        shares = shares + [swap_local(v, bit) for v in shares]
    for n, k in enumerate(hops):
        mine, other = (v[n % per * keep:(n % per + 1) * keep] for v in held[n // per])
        if k:
            total = add(mine, other)
            if n == nodes - 2:
                total = after(total, there)
            arrived[k] = lax.ppermute(total, "node", [(i, (i + k) % nodes) for i in range(nodes)])
        else:
            arrived[0] = (mine, other)
    d_tokens = pl.pallas_call(
        collect_kernel,
        out_shape=jax.ShapeDtypeStruct((keep, nodes, width), BF16),
        in_specs=[pl.BlockSpec(memory_space=pltpu.VMEM)] * (nodes + 1),
        out_specs=pl.BlockSpec(memory_space=pltpu.VMEM),
        compiler_params=pltpu.CompilerParams(vmem_limit_bytes=VMEM_LIMIT),
        name="collect",
    )(*arrived[1:], *arrived[0])
    shares[-1] = after(shares[-1], d_tokens)
    shares = shares + [swap_local(v, bits[0]) for v in shares]

    grad_gate, grad_up = weight_grads(order, tokens, weights, counts, shares, [(block, block)] * locals_, acts, there, (0, 1), False)
    (grad_down,) = weight_grads(order, grads, weights, counts, shares, [(0, block)] * locals_, acts, there, (2,), True)
    return d_tokens[None, None], grad_gate[None], grad_up[None], grad_down[None]


def solution(mesh):
    return jax.shard_map(
        on_device,
        mesh=mesh,
        in_specs=(
            P("dp", "node", None, None, None),
            P("dp", "node", None, None, None),
            P("dp", "node", None, None),
            P("dp", "node", None),
            P("node", None, "local"),
            P("node", None, "local"),
            P("node", None, "local"),
        ),
        out_specs=(
            P("dp", "node", "local", None, None),
            P("node", "dp", "local"),
            P("node", "dp", "local"),
            P("node", "dp", "local"),
        ),
        check_vma=False,
    )
```

```python
import functools

import jax
import jax.numpy as jnp
from jax import lax
from jax.experimental import pallas as pl
from jax.experimental.pallas import tpu as pltpu
from jax.sharding import PartitionSpec as P

F32, BF16 = jnp.float32, jnp.bfloat16
MIB = 1024 * 1024
VMEM_LIMIT = 24 * MIB
VMEM = 58 * MIB
FORWARD_LIMIT = 51 * MIB


def dot(a, b, contract_a, contract_b):
    return lax.dot_general(a, b, (((contract_a,), (contract_b,)), ((), ())), preferred_element_type=F32)


def flat_rows(block):
    return block.reshape(block.shape[0] * block.shape[1], block.shape[2])


def log2(n):
    assert n & (n - 1) == 0
    return n.bit_length() - 1


def halving_order(size):
    order = [0]
    for i in reversed(range(log2(size))):
        order = order + [d ^ (1 << i) for d in order]
    return order


def bit_reverse(value, bits):
    out = jnp.zeros_like(value)
    for i in range(bits):
        out = out | (((value >> i) & 1) << (bits - 1 - i))
    return out


def shift_order(nodes):
    return sorted(range(1, nodes), key=lambda k: (-min(k, nodes - k), k)) + [0]


def column(weights, counts, first, out_rows):
    weights = weights.T
    slots, nodes = weights.shape
    slot = first + lax.broadcasted_iota(jnp.int32, (slots, nodes), 0)
    factor = weights * jnp.where(slot < counts, 1.0, 0.0)
    spread = jnp.broadcast_to(factor[:, None, :], (slots, nodes, nodes)).reshape(out_rows, nodes)
    row = lax.broadcasted_iota(jnp.int32, (out_rows, nodes), 0)
    lane = lax.broadcasted_iota(jnp.int32, (out_rows, nodes), 1)
    return jnp.sum(jnp.where((row & (nodes - 1)) == lane, spread, 0.0), axis=1, keepdims=True)


def pick_slots(weights, first, keep):
    out = weights[:, :keep]
    for at in range(keep, weights.shape[1], keep):
        out = jnp.where(first == at, weights[:, at:at + keep], out)
    return out


def share_kernel(blocks, tok_hbm, grad_hbm, weights_hbm, counts_hbm, out, tok, grad, weights, counts, sem):
    keep, nodes, part = tok.shape
    me, other = lax.axis_index("local"), 1 - lax.axis_index("dp")
    cols = pl.ds(pl.multiple_of(other * part, 128), part)
    firsts = [(me ^ d) * keep for d in blocks]
    copies = [pltpu.make_async_copy(grad_hbm.at[pl.ds(first, keep), :, cols], grad.at[b], sem.at[b]) for b, first in enumerate(firsts)]
    copies.append(pltpu.make_async_copy(tok_hbm.at[pl.ds(firsts[0], keep), :, cols], tok, sem.at[len(blocks)]))
    small = [pltpu.make_async_copy(weights_hbm, weights, sem.at[len(blocks) + 1]),
             pltpu.make_async_copy(counts_hbm, counts, sem.at[len(blocks) + 2])]
    for copy in small + copies:
        copy.start()
    rows = keep * nodes
    for copy in small:
        copy.wait()
    for b, first in enumerate(firsts):
        factor = column(pick_slots(weights[...], first, keep), counts[...], first, rows)
        copies[b].wait()
        out[b * rows:(b + 1) * rows] = (flat_rows(grad[b].astype(F32)) * factor).astype(BF16)
    copies[-1].wait()
    out[len(blocks) * rows:] = flat_rows(tok[...])


def share(order, tokens, grads, weights, counts):
    slots, nodes, width = tokens.shape
    keep, part = slots // len(order), width // 2
    blocks = order[:1]
    vmem, hbm = pl.BlockSpec(memory_space=pltpu.VMEM), pl.BlockSpec(memory_space=pltpu.HBM)
    return pl.pallas_call(
        functools.partial(share_kernel, blocks),
        out_shape=jax.ShapeDtypeStruct(((len(blocks) + 1) * keep * nodes, part), BF16),
        in_specs=[hbm] * 4,
        out_specs=vmem,
        scratch_shapes=[pltpu.VMEM((keep, nodes, part), BF16), pltpu.VMEM((len(blocks), keep, nodes, part), BF16),
                        pltpu.VMEM(weights.shape, F32), pltpu.VMEM(counts.shape, jnp.int32),
                        pltpu.SemaphoreType.DMA((len(blocks) + 3,))],
        compiler_params=pltpu.CompilerParams(vmem_limit_bytes=VMEM),
        name="share",
    )(tokens, grads, weights, counts)


def forward_kernel(locals_, chunk, tok_hbm, grad_hbm, weights_hbm, counts_hbm, wg_hbm, wu_hbm, wd_hbm,
                   acts, own_a, own_b, send_a, send_b,
                   tok, grad, weights, counts, wgu, wd, acc, acc_h, moved, sem):
    slots, nodes, width = tok.shape
    rows = slots * nodes
    keep = slots // locals_
    steps = width // chunk
    hid_local = wd.shape[1]
    me, node = lax.axis_index("local"), lax.axis_index("node")

    def fetch(i):
        cols = pl.ds(i * chunk, chunk)
        ends = [(tok_hbm.at[:, :, cols], tok.at[:, :, cols]), (wg_hbm.at[cols], wgu.at[cols, :hid_local]),
                (wu_hbm.at[cols], wgu.at[cols, hid_local:]), (grad_hbm.at[:, :, cols], grad.at[:, :, cols]), (wd_hbm.at[cols], wd.at[cols])]
        return [pltpu.make_async_copy(src, dst, sem.at[i, n]) for n, (src, dst) in enumerate(ends)]

    small = [pltpu.make_async_copy(weights_hbm, weights, sem.at[steps, 0]), pltpu.make_async_copy(counts_hbm, counts, sem.at[steps, 1])]
    copies = [fetch(i) for i in range(steps)]
    for group in [small] + copies:
        for copy in group:
            copy.start()
    for copy in small:
        copy.wait()
    factor = column(weights[...], counts[...], 0, rows)
    for i in range(steps):
        cols = pl.ds(i * chunk, chunk)
        for copy in copies[i][:3]:
            copy.wait()
        both = dot(flat_rows(tok[:, :, cols]), wgu[cols], 1, 0)
        for copy in copies[i][3:]:
            copy.wait()
        scaled = (flat_rows(grad[:, :, cols].astype(F32)) * factor).astype(BF16)
        back = dot(scaled, wd[cols], 1, 0)
        if i:
            acc[...] += both
            acc_h[...] += back
        else:
            acc[...] = both
            acc_h[...] = back

    band = 64

    def activate(i, carry):
        at = pl.ds(pl.multiple_of(i * band, band), band)
        gate, up, back = acc[at, :hid_local], acc[at, hid_local:], acc_h[at]
        sig = jax.nn.sigmoid(gate)
        act = gate * sig
        acts[2, at] = (act * up).astype(BF16)
        acts[0, at] = (back * up * sig * (1.0 + gate * (1.0 - sig))).astype(BF16)
        acts[1, at] = (back * act).astype(BF16)
        return carry

    lax.fori_loop(0, rows // band, activate, 0)

    per = nodes // 2
    p = lax.broadcasted_iota(jnp.int32, (rows, 1), 0)
    j = p & (keep - 1)
    at = log2(keep)
    quick = (p >> at) & (per - 1)
    at += log2(per)
    low = (p >> at) & (locals_ // 2 - 1)
    at += log2(locals_ // 2)
    group = (p >> at) & 1
    high = p >> (at + 1)
    place = bit_reverse(high * (locals_ // 2) + low, log2(locals_)) ^ me
    hop = jnp.zeros_like(p)
    for n, k in enumerate(shift_order(nodes)):
        hop = jnp.where(group * per + quick == n, k, hop)
    index = (place * keep + j) * nodes + ((node + hop) & (nodes - 1))
    one_hot = jnp.where(index == lax.broadcasted_iota(jnp.int32, (rows, rows), 1), 1.0, 0.0).astype(BF16)
    moved[:, :hid_local] = dot(one_hot, acts[0], 1, 0).astype(BF16)
    moved[:, hid_local:] = dot(one_hot, acts[1], 1, 0).astype(BF16)
    quarter = rows // 4
    for i in range(steps):
        cols = pl.ds(i * chunk, chunk)
        total = dot(moved[...], wgu[cols], 1, 1).astype(BF16)
        for n, out in enumerate((own_a, own_b, send_a, send_b)):
            out[:, cols] = total[n * quarter:(n + 1) * quarter]


def forward(locals_, tokens, grads, weights, counts, gate_weight, up_weight, down_weight):
    slots, nodes, width = tokens.shape
    rows = slots * nodes
    hid_local = gate_weight.shape[1]
    vmem, hbm = pl.BlockSpec(memory_space=pltpu.VMEM), pl.BlockSpec(memory_space=pltpu.HBM)
    chunk = 512
    return pl.pallas_call(
        functools.partial(forward_kernel, locals_, chunk),
        out_shape=[jax.ShapeDtypeStruct((3, rows, hid_local), BF16)] + [jax.ShapeDtypeStruct((rows // 4, width), BF16)] * 4,
        in_specs=[hbm] * 7,
        out_specs=[vmem] * 5,
        scratch_shapes=[
            pltpu.VMEM(tokens.shape, BF16), pltpu.VMEM(tokens.shape, BF16), pltpu.VMEM(weights.shape, F32),
            pltpu.VMEM(counts.shape, jnp.int32), pltpu.VMEM((width, 2 * hid_local), BF16), pltpu.VMEM((width, hid_local), BF16),
            pltpu.VMEM((rows, 2 * hid_local), F32), pltpu.VMEM((rows, hid_local), F32), pltpu.VMEM((rows, 2 * hid_local), BF16),
            pltpu.SemaphoreType.DMA((width // chunk + 1, 5))],
        compiler_params=pltpu.CompilerParams(vmem_limit_bytes=FORWARD_LIMIT),
        cost_estimate=pl.CostEstimate(flops=10 * rows * width * hid_local, bytes_accessed=18_000_000, transcendentals=0),
        name="forward",
    )(tokens, grads, weights, counts, gate_weight, up_weight, down_weight)


def own_kernel(tok, grad, weights_ref, counts_ref, acts, gate_out, up_out, down_out):
    slots, nodes, width = tok.shape
    part = gate_out.shape[0]
    replica = lax.axis_index("dp")
    factor = column(weights_ref[...], counts_ref[...], 0, slots * nodes)
    chunk = 896
    for i in range(part // chunk):
        cols = pl.ds(i * chunk, chunk)
        mine = pl.ds(pl.multiple_of(replica * part + i * chunk, 128), chunk)
        rows = flat_rows(tok[:, :, mine])
        gate_out[cols] = dot(rows, acts[0], 0, 0).astype(BF16)
        up_out[cols] = dot(rows, acts[1], 0, 0).astype(BF16)
        scaled = (flat_rows(grad[:, :, mine].astype(F32)) * factor).astype(BF16)
        down_out[cols] = dot(scaled, acts[2], 0, 0).astype(BF16)


def own_grads(tokens, grads, weights, counts, acts):
    slots, nodes, width = tokens.shape
    rows, hid_local = acts.shape[1:]
    part = width // 2
    vmem = pl.BlockSpec(memory_space=pltpu.VMEM)
    return pl.pallas_call(
        own_kernel,
        out_shape=[jax.ShapeDtypeStruct((part, hid_local), BF16)] * 3,
        in_specs=[vmem] * 5,
        out_specs=[vmem] * 3,
        compiler_params=pltpu.CompilerParams(vmem_limit_bytes=VMEM_LIMIT),
        cost_estimate=pl.CostEstimate(flops=6 * rows * part * hid_local, bytes_accessed=10_000_000, transcendentals=0),
        name="own_grads",
    )(tokens, grads, weights, counts, acts)


def weight_kernel(order, first, acts_at, *refs):
    count = len(acts_at)
    shares = refs[:len(order)]
    there_ref = refs[len(order)]
    parts = refs[len(order) + 1:len(order) + 1 + count]
    outs = refs[len(order) + 1 + count:len(order) + 1 + 2 * count]
    left, right, bufs, sem = refs[len(order) + 1 + 2 * count:]
    part = outs[0].shape[0]
    me = lax.axis_index("local")
    block = shares[0].shape[0] // 2
    for n, a in enumerate(acts_at):
        for b, d in enumerate(order):
            right[n, b * block:(b + 1) * block] = there_ref[a, pl.ds(pl.multiple_of((me ^ d) * block, block), block)]
    chunk = left.shape[1]
    copies = []
    for i in range(part // chunk):
        cols = pl.ds(i * chunk, chunk)
        for b, ref in enumerate(shares):
            left[b * block:(b + 1) * block] = ref[first:first + block, cols]
        for n, out in enumerate(outs):
            bufs[n, cols] = (dot(left[...], right[n], 0, 0) + parts[n][cols].astype(F32)).astype(BF16)
            copies.append(pltpu.make_async_copy(bufs.at[n, cols], out.at[cols], sem.at[i, n]))
            copies[-1].start()
    for copy in copies:
        copy.wait()


def weight_grads(order, shares, first, there, parts, acts_at):
    part = shares[0].shape[-1]
    rows, hid_local = there.shape[1:]
    count = len(acts_at)
    chunk = 896
    vmem = pl.BlockSpec(memory_space=pltpu.VMEM)
    return pl.pallas_call(
        functools.partial(weight_kernel, order, first, acts_at),
        out_shape=[jax.ShapeDtypeStruct((part, hid_local), BF16)] * count,
        in_specs=[vmem] * (1 + len(shares) + count),
        out_specs=[pl.BlockSpec(memory_space=pltpu.HBM)] * count,
        scratch_shapes=[pltpu.VMEM((rows, chunk), BF16), pltpu.VMEM((count, rows, hid_local), BF16),
                        pltpu.VMEM((count, part, hid_local), BF16), pltpu.SemaphoreType.DMA((part // chunk, count))],
        compiler_params=pltpu.CompilerParams(vmem_limit_bytes=VMEM_LIMIT),
        cost_estimate=pl.CostEstimate(flops=2 * rows * part * hid_local * count, bytes_accessed=4_000_000, transcendentals=0),
        name="weight_grads",
    )(*shares, there, *parts)


def collect_kernel(*refs):
    *arrived, kept, came, out = refs
    keep, nodes, width = out.shape
    node = lax.axis_index("node")
    last = (kept[...].astype(F32) + came[...].astype(F32)).astype(BF16)
    stacked = jnp.concatenate([last] + [a[...] for a in arrived], axis=0)
    rows = keep * nodes
    p = lax.broadcasted_iota(jnp.int32, (rows, rows), 0)
    source = ((node - (p & (nodes - 1))) & (nodes - 1)) * keep + (p >> log2(nodes))
    one_hot = jnp.where(source == lax.broadcasted_iota(jnp.int32, (rows, rows), 1), 1.0, 0.0).astype(BF16)
    out[...] = dot(one_hot, stacked, 1, 0).astype(BF16).reshape(out.shape)


def after(value, other):
    return lax.optimization_barrier((value, other))[0]


def add(a, b):
    return (a.astype(F32) + b.astype(F32)).astype(BF16)


def on_device(tokens_in, grad_rows, combine_weights, live_counts, w_gate, w_up, w_down):
    slots, nodes, width = tokens_in.shape[2:]
    replicas, locals_ = lax.axis_size("dp"), lax.axis_size("local")
    assert replicas == 2
    keep = slots // locals_
    tokens, grads, weights, counts = tokens_in[0, 0], grad_rows[0, 0], combine_weights[0, 0].T, live_counts[0]
    order = halving_order(locals_)
    bits = [1 << i for i in range(log2(locals_))]

    def swap_local(value, bit):
        return lax.ppermute(value, "local", [(i, i ^ bit) for i in range(locals_)])

    def swap_dp(value):
        return lax.ppermute(value, "dp", [(0, 1), (1, 0)])

    rows = slots * nodes
    block = rows // locals_
    first, weights = lax.optimization_barrier((share(order, tokens, grads, weights, counts), weights))
    first = swap_dp(first)
    acts, own_a, own_b, send_a, send_b = forward(locals_, tokens, grads, weights, counts, w_gate[0], w_up[0], w_down[0])
    there = swap_dp(acts)

    per = nodes // 2
    hops = shift_order(nodes)
    arrived = [None] * nodes
    send_a, send_b = after(send_a, first), after(send_b, first)
    held = [(own_a, swap_local(send_a, bits[0])), (own_b, swap_local(send_b, bits[0]))]
    for bit in bits[1:]:
        for g, (mine, other) in enumerate(held):
            half = mine.shape[0] // 2
            held[g] = (add(mine[:half], other[:half]), swap_local(add(mine[half:], other[half:]), bit))
    shares = [after(first, held[0][1])]
    for bit in reversed(bits[1:]):
        shares = shares + [swap_local(v, bit) for v in shares]
    parts = own_grads(tokens, grads, weights, counts, after(acts, held[1][0]))
    held[0] = (after(held[0][0], parts[0]), held[0][1])
    for n, k in enumerate(hops):
        mine, other = (v[n % per * keep:(n % per + 1) * keep] for v in held[n // per])
        if k:
            total = add(mine, other)
            arrived[k] = lax.ppermute(total, "node", [(i, (i + k) % nodes) for i in range(nodes)])
        else:
            arrived[0] = (mine, other)
    early = lax.optimization_barrier([arrived[k] for k in hops[:per]] + [there])
    for k, value in zip(hops[:per], early):
        arrived[k] = value
    d_tokens = pl.pallas_call(
        collect_kernel,
        out_shape=jax.ShapeDtypeStruct((keep, nodes, width), BF16),
        in_specs=[pl.BlockSpec(memory_space=pltpu.VMEM)] * (nodes + 1),
        out_specs=pl.BlockSpec(memory_space=pltpu.VMEM),
        compiler_params=pltpu.CompilerParams(vmem_limit_bytes=VMEM_LIMIT),
        name="collect",
    )(*arrived[1:], *arrived[0])

    shares[-1] = after(shares[-1], d_tokens)
    shares = shares + [swap_local(v, bits[0]) for v in shares]
    grad_gate, grad_up = weight_grads(order, shares, block, there, parts[:2], (0, 1))
    (grad_down,) = weight_grads(order, shares, 0, there, parts[2:], (2,))
    return d_tokens[None, None], grad_gate[None], grad_up[None], grad_down[None]


def solution(mesh):
    return jax.shard_map(
        on_device,
        mesh=mesh,
        in_specs=(
            P("dp", "node", None, None, None),
            P("dp", "node", None, None, None),
            P("dp", "node", None, None),
            P("dp", "node", None),
            P("node", None, "local"),
            P("node", None, "local"),
            P("node", None, "local"),
        ),
        out_specs=(
            P("dp", "node", "local", None, None),
            P("node", "dp", "local"),
            P("node", "dp", "local"),
            P("node", "dp", "local"),
        ),
        check_vma=False,
    )
```

```python
import functools

import jax
import jax.numpy as jnp
from jax import lax
from jax.experimental import pallas as pl
from jax.experimental.pallas import tpu as pltpu
from jax.sharding import PartitionSpec as P

F32, BF16 = jnp.float32, jnp.bfloat16
MIB = 1024 * 1024
VMEM_LIMIT = 24 * MIB
VMEM = 58 * MIB
FORWARD_LIMIT = 51 * MIB


def dot(a, b, contract_a, contract_b):
    return lax.dot_general(a, b, (((contract_a,), (contract_b,)), ((), ())), preferred_element_type=F32)


def flat_rows(block):
    return block.reshape(block.shape[0] * block.shape[1], block.shape[2])


def log2(n):
    assert n & (n - 1) == 0
    return n.bit_length() - 1


def halving_order(size):
    order = [0]
    for i in reversed(range(log2(size))):
        order = order + [d ^ (1 << i) for d in order]
    return order


def bit_reverse(value, bits):
    out = jnp.zeros_like(value)
    for i in range(bits):
        out = out | (((value >> i) & 1) << (bits - 1 - i))
    return out


def shift_order(nodes):
    return sorted(range(1, nodes), key=lambda k: (-min(k, nodes - k), k)) + [0]


def column(weights, counts, first, out_rows):
    weights = weights.T
    slots, nodes = weights.shape
    slot = first + lax.broadcasted_iota(jnp.int32, (slots, nodes), 0)
    factor = weights * jnp.where(slot < counts, 1.0, 0.0)
    spread = jnp.broadcast_to(factor[:, None, :], (slots, nodes, nodes)).reshape(out_rows, nodes)
    row = lax.broadcasted_iota(jnp.int32, (out_rows, nodes), 0)
    lane = lax.broadcasted_iota(jnp.int32, (out_rows, nodes), 1)
    return jnp.sum(jnp.where((row & (nodes - 1)) == lane, spread, 0.0), axis=1, keepdims=True)


def pick_slots(weights, first, keep):
    out = weights[:, :keep]
    for at in range(keep, weights.shape[1], keep):
        out = jnp.where(first == at, weights[:, at:at + keep], out)
    return out


def share_kernel(blocks, tok_hbm, grad_hbm, weights_hbm, counts_hbm, out, tok, grad, weights, counts, sem):
    keep, nodes, part = tok.shape
    me, other = lax.axis_index("local"), 1 - lax.axis_index("dp")
    cols = pl.ds(pl.multiple_of(other * part, 128), part)
    firsts = [(me ^ d) * keep for d in blocks]
    copies = [pltpu.make_async_copy(grad_hbm.at[pl.ds(first, keep), :, cols], grad.at[b], sem.at[b]) for b, first in enumerate(firsts)]
    copies.append(pltpu.make_async_copy(tok_hbm.at[pl.ds(firsts[0], keep), :, cols], tok, sem.at[len(blocks)]))
    small = [pltpu.make_async_copy(weights_hbm, weights, sem.at[len(blocks) + 1]),
             pltpu.make_async_copy(counts_hbm, counts, sem.at[len(blocks) + 2])]
    for copy in small + copies:
        copy.start()
    rows = keep * nodes
    for copy in small:
        copy.wait()
    for b, first in enumerate(firsts):
        factor = column(pick_slots(weights[...], first, keep), counts[...], first, rows)
        copies[b].wait()
        out[b * rows:(b + 1) * rows] = (flat_rows(grad[b].astype(F32)) * factor).astype(BF16)
    copies[-1].wait()
    out[len(blocks) * rows:] = flat_rows(tok[...])


def share(order, tokens, grads, weights, counts):
    slots, nodes, width = tokens.shape
    keep, part = slots // len(order), width // 2
    blocks = order[:1]
    vmem, hbm = pl.BlockSpec(memory_space=pltpu.VMEM), pl.BlockSpec(memory_space=pltpu.HBM)
    return pl.pallas_call(
        functools.partial(share_kernel, blocks),
        out_shape=jax.ShapeDtypeStruct(((len(blocks) + 1) * keep * nodes, part), BF16),
        in_specs=[hbm] * 4,
        out_specs=vmem,
        scratch_shapes=[pltpu.VMEM((keep, nodes, part), BF16), pltpu.VMEM((len(blocks), keep, nodes, part), BF16),
                        pltpu.VMEM(weights.shape, F32), pltpu.VMEM(counts.shape, jnp.int32),
                        pltpu.SemaphoreType.DMA((len(blocks) + 3,))],
        compiler_params=pltpu.CompilerParams(vmem_limit_bytes=VMEM),
        name="share",
    )(tokens, grads, weights, counts)


def forward_kernel(locals_, chunk, tok_hbm, grad_hbm, weights_hbm, counts_hbm, wg_hbm, wu_hbm, wd_hbm,
                   acts, own_a, own_b, send_a_low, send_a_high, send_b_low, send_b_high,
                   tok, grad, weights, counts, wgu, wd, acc, acc_h, moved, sem):
    slots, nodes, width = tok.shape
    rows = slots * nodes
    keep = slots // locals_
    steps = width // chunk
    hid_local = wd.shape[1]
    me, node = lax.axis_index("local"), lax.axis_index("node")

    def fetch(i):
        cols = pl.ds(i * chunk, chunk)
        ends = [(tok_hbm.at[:, :, cols], tok.at[:, :, cols]), (wg_hbm.at[cols], wgu.at[cols, :hid_local]),
                (wu_hbm.at[cols], wgu.at[cols, hid_local:]), (grad_hbm.at[:, :, cols], grad.at[:, :, cols]), (wd_hbm.at[cols], wd.at[cols])]
        return [pltpu.make_async_copy(src, dst, sem.at[i, n]) for n, (src, dst) in enumerate(ends)]

    small = [pltpu.make_async_copy(weights_hbm, weights, sem.at[steps, 0]), pltpu.make_async_copy(counts_hbm, counts, sem.at[steps, 1])]
    copies = [fetch(i) for i in range(steps)]
    for group in [small] + copies:
        for copy in group:
            copy.start()
    for copy in small:
        copy.wait()
    factor = column(weights[...], counts[...], 0, rows)
    for i in range(steps):
        cols = pl.ds(i * chunk, chunk)
        for copy in copies[i][:3]:
            copy.wait()
        both = dot(flat_rows(tok[:, :, cols]), wgu[cols], 1, 0)
        for copy in copies[i][3:]:
            copy.wait()
        scaled = (flat_rows(grad[:, :, cols].astype(F32)) * factor).astype(BF16)
        back = dot(scaled, wd[cols], 1, 0)
        if i:
            acc[...] += both
            acc_h[...] += back
        else:
            acc[...] = both
            acc_h[...] = back

    band = 64

    def activate(i, carry):
        at = pl.ds(pl.multiple_of(i * band, band), band)
        gate, up, back = acc[at, :hid_local], acc[at, hid_local:], acc_h[at]
        sig = jax.nn.sigmoid(gate)
        act = gate * sig
        acts[2, at] = (act * up).astype(BF16)
        acts[0, at] = (back * up * sig * (1.0 + gate * (1.0 - sig))).astype(BF16)
        acts[1, at] = (back * act).astype(BF16)
        return carry

    lax.fori_loop(0, rows // band, activate, 0)

    per = nodes // 2
    p = lax.broadcasted_iota(jnp.int32, (rows, 1), 0)
    j = p & (keep - 1)
    at = log2(keep)
    quick = (p >> at) & (per - 1)
    at += log2(per)
    low = (p >> at) & (locals_ // 2 - 1)
    at += log2(locals_ // 2)
    group = (p >> at) & 1
    high = p >> (at + 1)
    place = bit_reverse(high * (locals_ // 2) + low, log2(locals_)) ^ me
    hop = jnp.zeros_like(p)
    for n, k in enumerate(shift_order(nodes)):
        hop = jnp.where(group * per + quick == n, k, hop)
    index = (place * keep + j) * nodes + ((node + hop) & (nodes - 1))
    one_hot = jnp.where(index == lax.broadcasted_iota(jnp.int32, (rows, rows), 1), 1.0, 0.0).astype(BF16)
    moved[:, :hid_local] = dot(one_hot, acts[0], 1, 0).astype(BF16)
    moved[:, hid_local:] = dot(one_hot, acts[1], 1, 0).astype(BF16)
    for i in range(steps):
        cols = pl.ds(i * chunk, chunk)
        total = dot(moved[...], wgu[cols], 1, 1).astype(BF16)
        at = 0
        for out in (own_a, own_b, send_a_low, send_a_high, send_b_low, send_b_high):
            out[:, cols] = total[at:at + out.shape[0]]
            at += out.shape[0]


def forward(locals_, tokens, grads, weights, counts, gate_weight, up_weight, down_weight):
    slots, nodes, width = tokens.shape
    rows = slots * nodes
    hid_local = gate_weight.shape[1]
    vmem, hbm = pl.BlockSpec(memory_space=pltpu.VMEM), pl.BlockSpec(memory_space=pltpu.HBM)
    chunk = 512
    return pl.pallas_call(
        functools.partial(forward_kernel, locals_, chunk),
        out_shape=[jax.ShapeDtypeStruct((3, rows, hid_local), BF16)] + [jax.ShapeDtypeStruct((rows // 4, width), BF16)] * 2
        + [jax.ShapeDtypeStruct((rows // 8, width), BF16)] * 4,
        in_specs=[hbm] * 7,
        out_specs=[vmem] * 7,
        scratch_shapes=[
            pltpu.VMEM(tokens.shape, BF16), pltpu.VMEM(tokens.shape, BF16), pltpu.VMEM(weights.shape, F32),
            pltpu.VMEM(counts.shape, jnp.int32), pltpu.VMEM((width, 2 * hid_local), BF16), pltpu.VMEM((width, hid_local), BF16),
            pltpu.VMEM((rows, 2 * hid_local), F32), pltpu.VMEM((rows, hid_local), F32), pltpu.VMEM((rows, 2 * hid_local), BF16),
            pltpu.SemaphoreType.DMA((width // chunk + 1, 5))],
        compiler_params=pltpu.CompilerParams(vmem_limit_bytes=FORWARD_LIMIT),
        cost_estimate=pl.CostEstimate(flops=10 * rows * width * hid_local, bytes_accessed=18_000_000, transcendentals=0),
        name="forward",
    )(tokens, grads, weights, counts, gate_weight, up_weight, down_weight)


def own_kernel(tok, grad, weights_ref, counts_ref, acts, gate_out, up_out, down_out):
    slots, nodes, width = tok.shape
    part = gate_out.shape[0]
    replica = lax.axis_index("dp")
    factor = column(weights_ref[...], counts_ref[...], 0, slots * nodes)
    chunk = 896
    for i in range(part // chunk):
        cols = pl.ds(i * chunk, chunk)
        mine = pl.ds(pl.multiple_of(replica * part + i * chunk, 128), chunk)
        rows = flat_rows(tok[:, :, mine])
        gate_out[cols] = dot(rows, acts[0], 0, 0).astype(BF16)
        up_out[cols] = dot(rows, acts[1], 0, 0).astype(BF16)
        scaled = (flat_rows(grad[:, :, mine].astype(F32)) * factor).astype(BF16)
        down_out[cols] = dot(scaled, acts[2], 0, 0).astype(BF16)


def own_grads(tokens, grads, weights, counts, acts):
    slots, nodes, width = tokens.shape
    rows, hid_local = acts.shape[1:]
    part = width // 2
    vmem = pl.BlockSpec(memory_space=pltpu.VMEM)
    return pl.pallas_call(
        own_kernel,
        out_shape=[jax.ShapeDtypeStruct((part, hid_local), BF16)] * 3,
        in_specs=[vmem] * 5,
        out_specs=[vmem] * 3,
        compiler_params=pltpu.CompilerParams(vmem_limit_bytes=VMEM_LIMIT),
        cost_estimate=pl.CostEstimate(flops=6 * rows * part * hid_local, bytes_accessed=10_000_000, transcendentals=0),
        name="own_grads",
    )(tokens, grads, weights, counts, acts)


def weight_kernel(order, *refs):
    shares = refs[:len(order)]
    there_ref, *parts = refs[len(order):len(order) + 4]
    outs = refs[len(order) + 4:len(order) + 7]
    left, right, bufs, sem = refs[len(order) + 7:]
    part = outs[0].shape[0]
    me = lax.axis_index("local")
    block = shares[0].shape[0] // 2
    for b, d in enumerate(order):
        right[:, b * block:(b + 1) * block] = there_ref[:, pl.ds(pl.multiple_of((me ^ d) * block, block), block)]
    chunk = left.shape[2]
    copies = []
    for i in range(part // chunk):
        cols = pl.ds(i * chunk, chunk)
        for b, ref in enumerate(shares):
            left[0, b * block:(b + 1) * block] = ref[block:, cols]
            left[1, b * block:(b + 1) * block] = ref[:block, cols]
        for n, out in enumerate(outs):
            bufs[n, cols] = (dot(left[n // 2], right[n], 0, 0) + parts[n][cols].astype(F32)).astype(BF16)
            copies.append(pltpu.make_async_copy(bufs.at[n, cols], out.at[cols], sem.at[i, n]))
            copies[-1].start()
    for copy in copies:
        copy.wait()


def weight_grads(order, shares, there, parts):
    part = shares[0].shape[-1]
    count, rows, hid_local = there.shape
    chunk = 896
    vmem = pl.BlockSpec(memory_space=pltpu.VMEM)
    return pl.pallas_call(
        functools.partial(weight_kernel, order),
        out_shape=[jax.ShapeDtypeStruct((part, hid_local), BF16)] * count,
        in_specs=[vmem] * (1 + len(shares) + count),
        out_specs=[pl.BlockSpec(memory_space=pltpu.HBM)] * count,
        scratch_shapes=[pltpu.VMEM((2, rows, chunk), BF16), pltpu.VMEM((count, rows, hid_local), BF16),
                        pltpu.VMEM((count, part, hid_local), BF16), pltpu.SemaphoreType.DMA((part // chunk, count))],
        compiler_params=pltpu.CompilerParams(vmem_limit_bytes=VMEM_LIMIT),
        cost_estimate=pl.CostEstimate(flops=2 * rows * part * hid_local * count, bytes_accessed=4_000_000, transcendentals=0),
        name="weight_grads",
    )(*shares, there, *parts)


def collect_kernel(*refs):
    *arrived, kept, came, out = refs
    keep, nodes, width = out.shape
    node = lax.axis_index("node")
    last = (kept[...].astype(F32) + came[...].astype(F32)).astype(BF16)
    stacked = jnp.concatenate([last] + [a[...] for a in arrived], axis=0)
    rows = keep * nodes
    p = lax.broadcasted_iota(jnp.int32, (rows, rows), 0)
    source = ((node - (p & (nodes - 1))) & (nodes - 1)) * keep + (p >> log2(nodes))
    one_hot = jnp.where(source == lax.broadcasted_iota(jnp.int32, (rows, rows), 1), 1.0, 0.0).astype(BF16)
    out[...] = dot(one_hot, stacked, 1, 0).astype(BF16).reshape(out.shape)


def after(value, other):
    return lax.optimization_barrier((value, other))[0]


def add(a, b):
    return (a.astype(F32) + b.astype(F32)).astype(BF16)


def on_device(tokens_in, grad_rows, combine_weights, live_counts, w_gate, w_up, w_down):
    slots, nodes, width = tokens_in.shape[2:]
    replicas, locals_ = lax.axis_size("dp"), lax.axis_size("local")
    assert replicas == 2
    keep = slots // locals_
    tokens, grads, weights, counts = tokens_in[0, 0], grad_rows[0, 0], combine_weights[0, 0].T, live_counts[0]
    order = halving_order(locals_)
    bits = [1 << i for i in range(log2(locals_))]

    def swap_local(value, bit):
        return lax.ppermute(value, "local", [(i, i ^ bit) for i in range(locals_)])

    def swap_dp(value):
        return lax.ppermute(value, "dp", [(0, 1), (1, 0)])

    rows = slots * nodes
    block = rows // locals_
    first, weights = lax.optimization_barrier((share(order, tokens, grads, weights, counts), weights))
    first = swap_dp(first)
    acts, own_a, own_b, *send = forward(locals_, tokens, grads, weights, counts, w_gate[0], w_up[0], w_down[0])
    there = swap_dp(acts)

    per = nodes // 2
    hops = shift_order(nodes)
    arrived = [None] * nodes
    low_a, high_a, low_b, high_b = send
    came = [swap_local(v, bits[0]) for v in (high_a, high_b, low_a, low_b)]
    came[0] = after(came[0], first)
    held = []
    for own, high, low in ((own_a, came[0], came[2]), (own_b, came[1], came[3])):
        half = own.shape[0] // 2
        held.append((add(own[:half], low), swap_local(add(own[half:], high), bits[1])))
    for bit in bits[2:]:
        for g, (mine, other) in enumerate(held):
            half = mine.shape[0] // 2
            held[g] = (add(mine[:half], other[:half]), swap_local(add(mine[half:], other[half:]), bit))
    shares = [after(first, held[0][1])]
    for bit in reversed(bits[1:]):
        shares = shares + [swap_local(v, bit) for v in shares]
    parts = own_grads(tokens, grads, weights, counts, after(acts, held[0][0]))
    held[0] = (after(held[0][0], parts[0]), held[0][1])
    for n, k in enumerate(hops):
        mine, other = (v[n % per * keep:(n % per + 1) * keep] for v in held[n // per])
        if k:
            total = add(mine, other)
            arrived[k] = lax.ppermute(total, "node", [(i, (i + k) % nodes) for i in range(nodes)])
        else:
            arrived[0] = (mine, other)
    early = lax.optimization_barrier([arrived[k] for k in hops[:per]] + [there])
    for k, value in zip(hops[:per], early):
        arrived[k] = value
    d_tokens = pl.pallas_call(
        collect_kernel,
        out_shape=jax.ShapeDtypeStruct((keep, nodes, width), BF16),
        in_specs=[pl.BlockSpec(memory_space=pltpu.VMEM)] * (nodes + 1),
        out_specs=pl.BlockSpec(memory_space=pltpu.VMEM),
        compiler_params=pltpu.CompilerParams(vmem_limit_bytes=VMEM_LIMIT),
        name="collect",
    )(*arrived[1:], *arrived[0])

    shares[-1] = after(shares[-1], d_tokens)
    shares = shares + [swap_local(v, bits[0]) for v in shares]
    grad_gate, grad_up, grad_down = weight_grads(order, shares, there, parts)
    return d_tokens[None, None], grad_gate[None], grad_up[None], grad_down[None]


def solution(mesh):
    return jax.shard_map(
        on_device,
        mesh=mesh,
        in_specs=(
            P("dp", "node", None, None, None),
            P("dp", "node", None, None, None),
            P("dp", "node", None, None),
            P("dp", "node", None),
            P("node", None, "local"),
            P("node", None, "local"),
            P("node", None, "local"),
        ),
        out_specs=(
            P("dp", "node", "local", None, None),
            P("node", "dp", "local"),
            P("node", "dp", "local"),
            P("node", "dp", "local"),
        ),
        check_vma=False,
    )
```

```python
import functools

import jax
import jax.numpy as jnp
from jax import lax
from jax.experimental import pallas as pl
from jax.experimental.pallas import tpu as pltpu
from jax.sharding import PartitionSpec as P

F32, BF16 = jnp.float32, jnp.bfloat16
MIB = 1024 * 1024
VMEM_LIMIT = 32 * MIB
TAIL, PIECE = 16, 256


def dot(a, b, contract_a, contract_b):
    return lax.dot_general(a, b, (((contract_a,), (contract_b,)), ((), ())), preferred_element_type=F32)


def flat_rows(block):
    return block.reshape(block.shape[0] * block.shape[1], block.shape[2])


def in_hbm(*arrays):
    return [pltpu.with_memory_space_constraint(a, pltpu.HBM) for a in arrays]


def log2(n):
    assert n & (n - 1) == 0
    return n.bit_length() - 1


def halving_order(size):
    order = [0]
    for i in reversed(range(log2(size))):
        order = order + [d ^ (1 << i) for d in order]
    return order


def bit_reverse(value, bits):
    out = jnp.zeros_like(value)
    for i in range(bits):
        out = out | (((value >> i) & 1) << (bits - 1 - i))
    return out


def shift_order(nodes):
    return sorted(range(1, nodes), key=lambda k: (-min(k, nodes - k), k)) + [0]


def column(weights, counts, first, out_rows):
    weights = weights.T
    slots, nodes = weights.shape
    slot = first + lax.broadcasted_iota(jnp.int32, (slots, nodes), 0)
    factor = weights * jnp.where(slot < counts, 1.0, 0.0)
    spread = jnp.broadcast_to(factor[:, None, :], (slots, nodes, nodes)).reshape(out_rows, nodes)
    row = lax.broadcasted_iota(jnp.int32, (out_rows, nodes), 0)
    lane = lax.broadcasted_iota(jnp.int32, (out_rows, nodes), 1)
    return jnp.sum(jnp.where((row & (nodes - 1)) == lane, spread, 0.0), axis=1, keepdims=True)


def pick_slots(weights, first, keep):
    out = weights[:, :keep]
    for at in range(keep, weights.shape[1], keep):
        out = jnp.where(first == at, weights[:, at:at + keep], out)
    return out


def share_kernel(tok_hbm, grad_hbm, weights_hbm, counts_hbm, out, tok, grad, weights, counts, sem):
    keep, nodes, part = tok.shape
    head = grad.shape[0]
    me, other = lax.axis_index("local"), 1 - lax.axis_index("dp")
    cols = pl.ds(pl.multiple_of(other * part, 128), part)
    first = me * keep
    copies = [pltpu.make_async_copy(weights_hbm, weights, sem.at[0]), pltpu.make_async_copy(counts_hbm, counts, sem.at[1]),
              pltpu.make_async_copy(grad_hbm.at[pl.ds(first, head), :, cols], grad, sem.at[2]),
              pltpu.make_async_copy(tok_hbm.at[pl.ds(first, keep), :, cols], tok, sem.at[3])]
    for copy in copies:
        copy.start()
    for copy in copies[:2]:
        copy.wait()
    factor = column(pick_slots(weights[...], first, keep), counts[...], first, keep * nodes)
    copies[2].wait()
    out[keep * nodes:] = (flat_rows(grad[...].astype(F32)) * factor[:head * nodes]).astype(BF16)
    copies[3].wait()
    out[:keep * nodes] = flat_rows(tok[...])


def share(locals_, tokens, grads, weights, counts):
    slots, nodes, width = tokens.shape
    keep, part = slots // locals_, width // 2
    head = keep - TAIL // nodes
    vmem, hbm = pl.BlockSpec(memory_space=pltpu.VMEM), pl.BlockSpec(memory_space=pltpu.HBM)
    return pl.pallas_call(
        share_kernel,
        out_shape=jax.ShapeDtypeStruct(((keep + head) * nodes, part), BF16),
        in_specs=[hbm] * 4,
        out_specs=vmem,
        scratch_shapes=[pltpu.VMEM((keep, nodes, part), BF16), pltpu.VMEM((head, nodes, part), BF16),
                        pltpu.VMEM(weights.shape, F32), pltpu.VMEM(counts.shape, jnp.int32), pltpu.SemaphoreType.DMA((4,))],
        compiler_params=pltpu.CompilerParams(vmem_limit_bytes=VMEM_LIMIT),
        name="share",
    )(*in_hbm(tokens, grads, weights, counts))


def tail_rows(part, hid_local, blocks):
    return -(-blocks * (part // PIECE) // (hid_local // PIECE)) * TAIL


def tail_spot(i, hid_local):
    across = hid_local // PIECE
    return slice(i // across * TAIL, (i // across + 1) * TAIL), slice(i % across * PIECE, (i % across + 1) * PIECE)


def forward_kernel(locals_, chunk, tok_hbm, grad_hbm, weights_hbm, counts_hbm, wg, wu_hbm, wd_hbm,
                   acts, own_a, own_b, send_a_low, send_a_high, send_b_low, send_b_high,
                   tok, grad, weights, counts, wu, wd, acc, acc_h, moved, sem):
    slots, nodes, width = tok.shape
    rows = slots * nodes
    keep = slots // locals_
    steps = width // chunk
    hid_local = wd.shape[1]
    me, node = lax.axis_index("local"), lax.axis_index("node")

    def fetch(i):
        cols = pl.ds(i * chunk, chunk)
        ends = [(tok_hbm.at[:, :, cols], tok.at[:, :, cols]), (wu_hbm.at[cols], wu.at[cols]), (grad_hbm.at[:, :, cols], grad.at[:, :, cols]), (wd_hbm.at[cols], wd.at[cols])]
        return [pltpu.make_async_copy(src, dst, sem.at[i, n]) for n, (src, dst) in enumerate(ends)]

    small = [pltpu.make_async_copy(weights_hbm, weights, sem.at[steps, 0]), pltpu.make_async_copy(counts_hbm, counts, sem.at[steps, 1])]
    copies = [fetch(i) for i in range(steps)]
    for group in [small] + copies:
        for copy in group:
            copy.start()
    for copy in small:
        copy.wait()
    factor = column(weights[...], counts[...], 0, rows)
    for i in range(steps):
        cols = pl.ds(i * chunk, chunk)
        copies[i][0].wait()
        t = flat_rows(tok[:, :, cols])
        gate = dot(t, wg[cols], 1, 0)
        copies[i][1].wait()
        up = dot(t, wu[cols], 1, 0)
        for copy in copies[i][2:]:
            copy.wait()
        scaled = (flat_rows(grad[:, :, cols].astype(F32)) * factor).astype(BF16)
        back = dot(scaled, wd[cols], 1, 0)
        if i:
            acc[:, :hid_local] += gate
            acc[:, hid_local:] += up
            acc_h[...] += back
        else:
            acc[:, :hid_local] = gate
            acc[:, hid_local:] = up
            acc_h[...] = back

    part, block = width // 2, keep * nodes
    cols = pl.ds(pl.multiple_of((1 - lax.axis_index("dp")) * part, 128), part)
    pieces = part // PIECE
    for b, d in enumerate(halving_order(locals_)[:locals_ // 2]):
        place = me ^ d
        picked = jnp.zeros((TAIL, 1), F32)
        for n in range(locals_):
            picked = jnp.where(place == n, factor[(n + 1) * block - TAIL:(n + 1) * block], picked)
        slot = pl.ds((place + 1) * keep - TAIL // nodes, TAIL // nodes)
        tail = (flat_rows(grad[slot, :, cols].astype(F32)) * picked).astype(BF16)
        for i in range(pieces):
            down, across = tail_spot(b * pieces + i, hid_local)
            acts[3 * rows + down.start:3 * rows + down.stop, across] = tail[:, i * PIECE:(i + 1) * PIECE]

    band = 64

    def activate(i, carry):
        at = pl.ds(pl.multiple_of(i * band, band), band)
        gate, up, back = acc[at, :hid_local], acc[at, hid_local:], acc_h[at]
        sig = jax.nn.sigmoid(gate)
        act = gate * sig
        acts[pl.ds(pl.multiple_of(2 * rows + i * band, band), band)] = (act * up).astype(BF16)
        acts[at] = (back * up * sig * (1.0 + gate * (1.0 - sig))).astype(BF16)
        acts[pl.ds(pl.multiple_of(rows + i * band, band), band)] = (back * act).astype(BF16)
        return carry

    lax.fori_loop(0, rows // band, activate, 0)

    per = nodes // 2
    p = lax.broadcasted_iota(jnp.int32, (rows, 1), 0)
    j = p & (keep - 1)
    at = log2(keep)
    quick = (p >> at) & (per - 1)
    at += log2(per)
    low = (p >> at) & (locals_ // 2 - 1)
    at += log2(locals_ // 2)
    group = (p >> at) & 1
    high = p >> (at + 1)
    place = bit_reverse(high * (locals_ // 2) + low, log2(locals_)) ^ me
    hop = jnp.zeros_like(p)
    for n, k in enumerate(shift_order(nodes)):
        hop = jnp.where(group * per + quick == n, k, hop)
    index = (place * keep + j) * nodes + ((node + hop) & (nodes - 1))
    one_hot = jnp.where(index == lax.broadcasted_iota(jnp.int32, (rows, rows), 1), 1.0, 0.0).astype(BF16)
    moved[:, :hid_local] = dot(one_hot, acts[:rows], 1, 0).astype(BF16)
    moved[:, hid_local:] = dot(one_hot, acts[rows:2 * rows], 1, 0).astype(BF16)
    for i in range(steps):
        cols = pl.ds(i * chunk, chunk)
        total = (dot(moved[:, :hid_local], wg[cols], 1, 1) + dot(moved[:, hid_local:], wu[cols], 1, 1)).astype(BF16)
        at = 0
        for out in (own_a, own_b, send_a_low, send_a_high, send_b_low, send_b_high):
            out[:, cols] = total[at:at + out.shape[0]]
            at += out.shape[0]


def forward(locals_, tokens, grads, weights, counts, gate_weight, up_weight, down_weight):
    slots, nodes, width = tokens.shape
    rows = slots * nodes
    hid_local = gate_weight.shape[1]
    vmem, hbm = pl.BlockSpec(memory_space=pltpu.VMEM), pl.BlockSpec(memory_space=pltpu.HBM)
    chunk = 512
    return pl.pallas_call(
        functools.partial(forward_kernel, locals_, chunk),
        out_shape=[jax.ShapeDtypeStruct((3 * rows + tail_rows(width // 2, hid_local, locals_ // 2), hid_local), BF16)] + [jax.ShapeDtypeStruct((rows // 4, width), BF16)] * 2
        + [jax.ShapeDtypeStruct((rows // 8, width), BF16)] * 4,
        in_specs=[hbm] * 4 + [vmem] + [hbm] * 2,
        out_specs=[vmem] * 7,
        scratch_shapes=[
            pltpu.VMEM(tokens.shape, BF16), pltpu.VMEM(tokens.shape, BF16), pltpu.VMEM(weights.shape, F32),
            pltpu.VMEM(counts.shape, jnp.int32), pltpu.VMEM((width, hid_local), BF16), pltpu.VMEM((width, hid_local), BF16),
            pltpu.VMEM((rows, 2 * hid_local), F32), pltpu.VMEM((rows, hid_local), F32), pltpu.VMEM((rows, 2 * hid_local), BF16),
            pltpu.SemaphoreType.DMA((width // chunk + 1, 4))],
        compiler_params=pltpu.CompilerParams(vmem_limit_bytes=VMEM_LIMIT),
        cost_estimate=pl.CostEstimate(flops=10 * rows * width * hid_local, bytes_accessed=18_000_000, transcendentals=0),
        name="forward",
    )(*in_hbm(tokens, grads, weights, counts), gate_weight, *in_hbm(up_weight, down_weight))


def own_kernel(tok, grad, weights_ref, counts_ref, acts, gate_out, up_out, down_out):
    slots, nodes, width = tok.shape
    part = gate_out.shape[0]
    replica = lax.axis_index("dp")
    count = slots * nodes
    factor = column(weights_ref[...], counts_ref[...], 0, count)
    chunk = 896
    for i in range(part // chunk):
        cols = pl.ds(i * chunk, chunk)
        mine = pl.ds(pl.multiple_of(replica * part + i * chunk, 128), chunk)
        rows = flat_rows(tok[:, :, mine])
        gate_out[cols] = dot(rows, acts[:count], 0, 0).astype(BF16)
        up_out[cols] = dot(rows, acts[count:2 * count], 0, 0).astype(BF16)
        scaled = (flat_rows(grad[:, :, mine].astype(F32)) * factor).astype(BF16)
        down_out[cols] = dot(scaled, acts[2 * count:3 * count], 0, 0).astype(BF16)


def own_grads(tokens, grads, weights, counts, acts):
    slots, nodes, width = tokens.shape
    rows, hid_local = slots * nodes, acts.shape[1]
    part = width // 2
    vmem = pl.BlockSpec(memory_space=pltpu.VMEM)
    return pl.pallas_call(
        own_kernel,
        out_shape=[jax.ShapeDtypeStruct((part, hid_local), BF16)] * 3,
        in_specs=[vmem] * 5,
        out_specs=[vmem] * 3,
        compiler_params=pltpu.CompilerParams(vmem_limit_bytes=VMEM_LIMIT),
        cost_estimate=pl.CostEstimate(flops=6 * rows * part * hid_local, bytes_accessed=10_000_000, transcendentals=0),
        name="own_grads",
    )(tokens, grads, weights, counts, acts)


def weight_kernel(order, block, *refs):
    shares = refs[:len(order)]
    there_ref, tails_ref, *parts = refs[len(order):len(order) + 5]
    outs = refs[len(order) + 5:len(order) + 8]
    left, right, bufs, sem = refs[len(order) + 8:]
    part, hid_local = outs[0].shape
    me = lax.axis_index("local")
    rows = len(order) * block
    for b, d in enumerate(order):
        for n in range(3):
            right[n, b * block:(b + 1) * block] = there_ref[pl.ds(pl.multiple_of(n * rows + (me ^ d) * block, block), block)]
    pieces = part // PIECE
    half = len(order) // 2
    for b, ref in enumerate(shares):
        left[0, b * block:(b + 1) * block] = ref[:block]
        left[1, b * block:(b + 1) * block - TAIL] = ref[block:]
        source, first = (there_ref, 3 * rows) if b < half else (tails_ref, 0)
        for i in range(pieces):
            down, across = tail_spot(b % half * pieces + i, hid_local)
            left[1, (b + 1) * block - TAIL:(b + 1) * block, i * PIECE:(i + 1) * PIECE] = (
                source[first + down.start:first + down.stop, across])
    chunk = 896
    copies = []
    for i in range(part // chunk):
        cols = pl.ds(i * chunk, chunk)
        for n, out in enumerate(outs):
            bufs[n, cols] = (dot(left[n // 2, :, cols], right[n], 0, 0) + parts[n][cols].astype(F32)).astype(BF16)
            copies.append(pltpu.make_async_copy(bufs.at[n, cols], out.at[cols], sem.at[i, n]))
            copies[-1].start()
    for copy in copies:
        copy.wait()


def weight_grads(order, block, shares, there, tails, parts):
    part = shares[0].shape[-1]
    hid_local = there.shape[1]
    rows = len(order) * block
    vmem = pl.BlockSpec(memory_space=pltpu.VMEM)
    return pl.pallas_call(
        functools.partial(weight_kernel, order, block),
        out_shape=[jax.ShapeDtypeStruct((part, hid_local), BF16)] * 3,
        in_specs=[vmem] * (5 + len(shares)),
        out_specs=[pl.BlockSpec(memory_space=pltpu.HBM)] * 3,
        scratch_shapes=[pltpu.VMEM((2, rows, part), BF16), pltpu.VMEM((3, rows, hid_local), BF16),
                        pltpu.VMEM((3, part, hid_local), BF16), pltpu.SemaphoreType.DMA((part // 896, 3))],
        compiler_params=pltpu.CompilerParams(vmem_limit_bytes=VMEM_LIMIT),
        cost_estimate=pl.CostEstimate(flops=6 * rows * part * hid_local, bytes_accessed=4_000_000, transcendentals=0),
        name="weight_grads",
    )(*shares, there, tails, *parts)


def collect_kernel(*refs):
    *arrived, kept, came, out = refs
    keep, nodes, width = out.shape
    node = lax.axis_index("node")
    last = (kept[...].astype(F32) + came[...].astype(F32)).astype(BF16)
    stacked = jnp.concatenate([last] + [a[...] for a in arrived], axis=0)
    rows = keep * nodes
    p = lax.broadcasted_iota(jnp.int32, (rows, rows), 0)
    source = ((node - (p & (nodes - 1))) & (nodes - 1)) * keep + (p >> log2(nodes))
    one_hot = jnp.where(source == lax.broadcasted_iota(jnp.int32, (rows, rows), 1), 1.0, 0.0).astype(BF16)
    out[...] = dot(one_hot, stacked, 1, 0).astype(BF16).reshape(out.shape)


def after(value, other):
    return lax.optimization_barrier((value, other))[0]


def add(a, b):
    return (a.astype(F32) + b.astype(F32)).astype(BF16)


def on_device(tokens_in, grad_rows, combine_weights, live_counts, w_gate, w_up, w_down):
    slots, nodes, width = tokens_in.shape[2:]
    replicas, locals_ = lax.axis_size("dp"), lax.axis_size("local")
    assert replicas == 2
    keep = slots // locals_
    tokens, grads, weights, counts = tokens_in[0, 0], grad_rows[0, 0], combine_weights[0, 0].T, live_counts[0]
    order = halving_order(locals_)
    bits = [1 << i for i in range(log2(locals_))]

    def swap_local(value, bit):
        return lax.ppermute(value, "local", [(i, i ^ bit) for i in range(locals_)])

    def swap_dp(value):
        return lax.ppermute(value, "dp", [(0, 1), (1, 0)])

    rows = slots * nodes
    block = rows // locals_
    first, weights = lax.optimization_barrier((share(locals_, tokens, grads, weights, counts), weights))
    first = swap_dp(first)
    acts, own_a, own_b, *send = forward(locals_, tokens, grads, weights, counts, w_gate[0], w_up[0], w_down[0])
    there = swap_dp(acts)

    per = nodes // 2
    hops = shift_order(nodes)
    arrived = [None] * nodes
    low_a, high_a, low_b, high_b = send
    came = [swap_local(v, bits[0]) for v in (high_a, high_b, low_a, low_b)]
    came[0] = after(came[0], first)
    half = own_a.shape[0] // 2
    held = [(add(own_a[:half], came[2]), swap_local(add(own_a[half:], came[0]), bits[1]))]
    parts = own_grads(tokens, grads, weights, counts, after(acts, held[0][0]))
    held.append((add(own_b[:half], came[3]), swap_local(after(add(own_b[half:], came[1]), parts[0]), bits[1])))
    for bit in bits[2:]:
        for g, (mine, other) in enumerate(held):
            half = mine.shape[0] // 2
            held[g] = (add(mine[:half], other[:half]), swap_local(add(mine[half:], other[half:]), bit))
    shares = [after(first, held[0][1])]
    for bit in reversed(bits[1:]):
        shares = shares + [swap_local(v, bit) for v in shares]
    for n, k in enumerate(hops):
        mine, other = (v[n % per * keep:(n % per + 1) * keep] for v in held[n // per])
        if k:
            total = add(mine, other)
            arrived[k] = lax.ppermute(total, "node", [(i, (i + k) % nodes) for i in range(nodes)])
        else:
            arrived[0] = (mine, other)
    early = lax.optimization_barrier([arrived[k] for k in hops[:per]])
    for k, value in zip(hops[:per], early):
        arrived[k] = value
    d_tokens = pl.pallas_call(
        collect_kernel,
        out_shape=jax.ShapeDtypeStruct((keep, nodes, width), BF16),
        in_specs=[pl.BlockSpec(memory_space=pltpu.VMEM)] * (nodes + 1),
        out_specs=pl.BlockSpec(memory_space=pltpu.VMEM),
        compiler_params=pltpu.CompilerParams(vmem_limit_bytes=VMEM_LIMIT),
        name="collect",
    )(*arrived[1:], *arrived[0])

    shares[-1] = after(shares[-1], d_tokens)
    shares = shares + [swap_local(v, bits[0]) for v in shares]
    tails = swap_local(there[3 * rows:], bits[0])
    grad_gate, grad_up, grad_down = weight_grads(order, block, shares, there, tails, parts)
    return d_tokens[None, None], grad_gate[None], grad_up[None], grad_down[None]


def solution(mesh):
    return jax.shard_map(
        on_device,
        mesh=mesh,
        in_specs=(
            P("dp", "node", None, None, None),
            P("dp", "node", None, None, None),
            P("dp", "node", None, None),
            P("dp", "node", None),
            P("node", None, "local"),
            P("node", None, "local"),
            P("node", None, "local"),
        ),
        out_specs=(
            P("dp", "node", "local", None, None),
            P("node", "dp", "local"),
            P("node", "dp", "local"),
            P("node", "dp", "local"),
        ),
        check_vma=False,
    )
```

```python
import functools

import jax
import jax.numpy as jnp
from jax import lax
from jax.experimental import pallas as pl
from jax.experimental.pallas import tpu as pltpu
from jax.sharding import PartitionSpec as P

F32, BF16 = jnp.float32, jnp.bfloat16
MIB = 1024 * 1024
VMEM_LIMIT = 32 * MIB
TAIL, PIECE = 16, 256


def dot(a, b, contract_a, contract_b):
    return lax.dot_general(a, b, (((contract_a,), (contract_b,)), ((), ())), preferred_element_type=F32)


def flat_rows(block):
    return block.reshape(block.shape[0] * block.shape[1], block.shape[2])


def in_hbm(*arrays):
    return [pltpu.with_memory_space_constraint(a, pltpu.HBM) for a in arrays]


def log2(n):
    assert n & (n - 1) == 0
    return n.bit_length() - 1


def halving_order(size):
    order = [0]
    for i in reversed(range(log2(size))):
        order = order + [d ^ (1 << i) for d in order]
    return order


def bit_reverse(value, bits):
    out = jnp.zeros_like(value)
    for i in range(bits):
        out = out | (((value >> i) & 1) << (bits - 1 - i))
    return out


def hop_order(nodes):
    return sorted(range(1, nodes), key=lambda k: (-k.bit_length(), k)) + [0]


def column(weights, counts, first, out_rows):
    weights = weights.T
    slots, nodes = weights.shape
    slot = first + lax.broadcasted_iota(jnp.int32, (slots, nodes), 0)
    factor = weights * jnp.where(slot < counts, 1.0, 0.0)
    spread = jnp.broadcast_to(factor[:, None, :], (slots, nodes, nodes)).reshape(out_rows, nodes)
    row = lax.broadcasted_iota(jnp.int32, (out_rows, nodes), 0)
    lane = lax.broadcasted_iota(jnp.int32, (out_rows, nodes), 1)
    return jnp.sum(jnp.where((row & (nodes - 1)) == lane, spread, 0.0), axis=1, keepdims=True)


def pick_slots(weights, first, keep):
    out = weights[:, :keep]
    for at in range(keep, weights.shape[1], keep):
        out = jnp.where(first == at, weights[:, at:at + keep], out)
    return out


def share_kernel(tok_hbm, grad_hbm, weights_hbm, counts_hbm, out, tok, grad, weights, counts, sem):
    keep, nodes, part = tok.shape
    head = grad.shape[0]
    me, other = lax.axis_index("local"), 1 - lax.axis_index("dp")
    cols = pl.ds(pl.multiple_of(other * part, 128), part)
    first = me * keep
    copies = [pltpu.make_async_copy(weights_hbm, weights, sem.at[0]), pltpu.make_async_copy(counts_hbm, counts, sem.at[1]),
              pltpu.make_async_copy(grad_hbm.at[pl.ds(first, head), :, cols], grad, sem.at[2]),
              pltpu.make_async_copy(tok_hbm.at[pl.ds(first, keep), :, cols], tok, sem.at[3])]
    for copy in copies:
        copy.start()
    for copy in copies[:2]:
        copy.wait()
    factor = column(pick_slots(weights[...], first, keep), counts[...], first, keep * nodes)
    copies[2].wait()
    out[keep * nodes:] = (flat_rows(grad[...].astype(F32)) * factor[:head * nodes]).astype(BF16)
    copies[3].wait()
    out[:keep * nodes] = flat_rows(tok[...])


def share(locals_, tokens, grads, weights, counts):
    slots, nodes, width = tokens.shape
    keep, part = slots // locals_, width // 2
    head = keep - TAIL // nodes
    vmem, hbm = pl.BlockSpec(memory_space=pltpu.VMEM), pl.BlockSpec(memory_space=pltpu.HBM)
    return pl.pallas_call(
        share_kernel,
        out_shape=jax.ShapeDtypeStruct(((keep + head) * nodes, part), BF16),
        in_specs=[hbm] * 4,
        out_specs=vmem,
        scratch_shapes=[pltpu.VMEM((keep, nodes, part), BF16), pltpu.VMEM((head, nodes, part), BF16),
                        pltpu.VMEM(weights.shape, F32), pltpu.VMEM(counts.shape, jnp.int32), pltpu.SemaphoreType.DMA((4,))],
        compiler_params=pltpu.CompilerParams(vmem_limit_bytes=VMEM_LIMIT),
        name="share",
    )(*in_hbm(tokens, grads, weights, counts))


def tail_rows(part, hid_local, blocks):
    return -(-blocks * (part // PIECE) // (hid_local // PIECE)) * TAIL


def tail_spot(i, hid_local):
    across = hid_local // PIECE
    return slice(i // across * TAIL, (i // across + 1) * TAIL), slice(i % across * PIECE, (i % across + 1) * PIECE)


def forward_kernel(locals_, chunk, tok_hbm, grad_hbm, weights_hbm, counts_hbm, wg, wu_hbm, wd_hbm,
                   acts, own_a, own_b, send_a_low, send_a_high, send_b_low, send_b_high,
                   tok, grad, weights, counts, wu, wd, acc, acc_h, moved, sem):
    slots, nodes, width = tok.shape
    rows = slots * nodes
    keep = slots // locals_
    steps = width // chunk
    hid_local = wd.shape[1]
    me, node = lax.axis_index("local"), lax.axis_index("node")

    def fetch(i):
        cols = pl.ds(i * chunk, chunk)
        ends = [(tok_hbm.at[:, :, cols], tok.at[:, :, cols]), (wu_hbm.at[cols], wu.at[cols]), (grad_hbm.at[:, :, cols], grad.at[:, :, cols]), (wd_hbm.at[cols], wd.at[cols])]
        return [pltpu.make_async_copy(src, dst, sem.at[i, n]) for n, (src, dst) in enumerate(ends)]

    small = [pltpu.make_async_copy(weights_hbm, weights, sem.at[steps, 0]), pltpu.make_async_copy(counts_hbm, counts, sem.at[steps, 1])]
    copies = [fetch(i) for i in range(steps)]
    for group in [small] + copies:
        for copy in group:
            copy.start()
    for copy in small:
        copy.wait()
    factor = column(weights[...], counts[...], 0, rows)
    for i in range(steps):
        cols = pl.ds(i * chunk, chunk)
        copies[i][0].wait()
        t = flat_rows(tok[:, :, cols])
        gate = dot(t, wg[cols], 1, 0)
        copies[i][1].wait()
        up = dot(t, wu[cols], 1, 0)
        for copy in copies[i][2:]:
            copy.wait()
        scaled = (flat_rows(grad[:, :, cols].astype(F32)) * factor).astype(BF16)
        back = dot(scaled, wd[cols], 1, 0)
        if i:
            acc[:, :hid_local] += gate
            acc[:, hid_local:] += up
            acc_h[...] += back
        else:
            acc[:, :hid_local] = gate
            acc[:, hid_local:] = up
            acc_h[...] = back

    part, block = width // 2, keep * nodes
    cols = pl.ds(pl.multiple_of((1 - lax.axis_index("dp")) * part, 128), part)
    pieces = part // PIECE
    for b, d in enumerate(halving_order(locals_)[:locals_ // 2]):
        place = me ^ d
        picked = jnp.zeros((TAIL, 1), F32)
        for n in range(locals_):
            picked = jnp.where(place == n, factor[(n + 1) * block - TAIL:(n + 1) * block], picked)
        slot = pl.ds((place + 1) * keep - TAIL // nodes, TAIL // nodes)
        tail = (flat_rows(grad[slot, :, cols].astype(F32)) * picked).astype(BF16)
        for i in range(pieces):
            down, across = tail_spot(b * pieces + i, hid_local)
            acts[3 * rows + down.start:3 * rows + down.stop, across] = tail[:, i * PIECE:(i + 1) * PIECE]

    band = 64

    def activate(i, carry):
        at = pl.ds(pl.multiple_of(i * band, band), band)
        gate, up, back = acc[at, :hid_local], acc[at, hid_local:], acc_h[at]
        sig = jax.nn.sigmoid(gate)
        act = gate * sig
        acts[pl.ds(pl.multiple_of(2 * rows + i * band, band), band)] = (act * up).astype(BF16)
        acts[at] = (back * up * sig * (1.0 + gate * (1.0 - sig))).astype(BF16)
        acts[pl.ds(pl.multiple_of(rows + i * band, band), band)] = (back * act).astype(BF16)
        return carry

    lax.fori_loop(0, rows // band, activate, 0)

    per = nodes // 2
    p = lax.broadcasted_iota(jnp.int32, (rows, 1), 0)
    j = p & (keep - 1)
    at = log2(keep)
    quick = (p >> at) & (per - 1)
    at += log2(per)
    low = (p >> at) & (locals_ // 2 - 1)
    at += log2(locals_ // 2)
    group = (p >> at) & 1
    high = p >> (at + 1)
    place = bit_reverse(high * (locals_ // 2) + low, log2(locals_)) ^ me
    hop = jnp.zeros_like(p)
    for n, k in enumerate(hop_order(nodes)):
        hop = jnp.where(group * per + quick == n, k, hop)
    index = (place * keep + j) * nodes + (node ^ hop)
    one_hot = jnp.where(index == lax.broadcasted_iota(jnp.int32, (rows, rows), 1), 1.0, 0.0).astype(BF16)
    moved[:, :hid_local] = dot(one_hot, acts[:rows], 1, 0).astype(BF16)
    moved[:, hid_local:] = dot(one_hot, acts[rows:2 * rows], 1, 0).astype(BF16)
    for i in range(steps):
        cols = pl.ds(i * chunk, chunk)
        total = (dot(moved[:, :hid_local], wg[cols], 1, 1) + dot(moved[:, hid_local:], wu[cols], 1, 1)).astype(BF16)
        at = 0
        for out in (own_a, own_b, send_a_low, send_a_high, send_b_low, send_b_high):
            out[:, cols] = total[at:at + out.shape[0]]
            at += out.shape[0]


def forward(locals_, tokens, grads, weights, counts, gate_weight, up_weight, down_weight):
    slots, nodes, width = tokens.shape
    rows = slots * nodes
    hid_local = gate_weight.shape[1]
    vmem, hbm = pl.BlockSpec(memory_space=pltpu.VMEM), pl.BlockSpec(memory_space=pltpu.HBM)
    chunk = 512
    return pl.pallas_call(
        functools.partial(forward_kernel, locals_, chunk),
        out_shape=[jax.ShapeDtypeStruct((3 * rows + tail_rows(width // 2, hid_local, locals_ // 2), hid_local), BF16)] + [jax.ShapeDtypeStruct((rows // 4, width), BF16)] * 2
        + [jax.ShapeDtypeStruct((rows // 8, width), BF16)] * 4,
        in_specs=[hbm] * 4 + [vmem] + [hbm] * 2,
        out_specs=[vmem] * 7,
        scratch_shapes=[
            pltpu.VMEM(tokens.shape, BF16), pltpu.VMEM(tokens.shape, BF16), pltpu.VMEM(weights.shape, F32),
            pltpu.VMEM(counts.shape, jnp.int32), pltpu.VMEM((width, hid_local), BF16), pltpu.VMEM((width, hid_local), BF16),
            pltpu.VMEM((rows, 2 * hid_local), F32), pltpu.VMEM((rows, hid_local), F32), pltpu.VMEM((rows, 2 * hid_local), BF16),
            pltpu.SemaphoreType.DMA((width // chunk + 1, 4))],
        compiler_params=pltpu.CompilerParams(vmem_limit_bytes=VMEM_LIMIT),
        cost_estimate=pl.CostEstimate(flops=10 * rows * width * hid_local, bytes_accessed=18_000_000, transcendentals=0),
        name="forward",
    )(*in_hbm(tokens, grads, weights, counts), gate_weight, *in_hbm(up_weight, down_weight))


def own_kernel(tok, grad, weights_ref, counts_ref, acts, gate_out, up_out, down_out):
    slots, nodes, width = tok.shape
    part = gate_out.shape[0]
    replica = lax.axis_index("dp")
    count = slots * nodes
    factor = column(weights_ref[...], counts_ref[...], 0, count)
    chunk = 896
    for i in range(part // chunk):
        cols = pl.ds(i * chunk, chunk)
        mine = pl.ds(pl.multiple_of(replica * part + i * chunk, 128), chunk)
        rows = flat_rows(tok[:, :, mine])
        gate_out[cols] = dot(rows, acts[:count], 0, 0).astype(BF16)
        up_out[cols] = dot(rows, acts[count:2 * count], 0, 0).astype(BF16)
        scaled = (flat_rows(grad[:, :, mine].astype(F32)) * factor).astype(BF16)
        down_out[cols] = dot(scaled, acts[2 * count:3 * count], 0, 0).astype(BF16)


def own_grads(tokens, grads, weights, counts, acts):
    slots, nodes, width = tokens.shape
    rows, hid_local = slots * nodes, acts.shape[1]
    part = width // 2
    vmem = pl.BlockSpec(memory_space=pltpu.VMEM)
    return pl.pallas_call(
        own_kernel,
        out_shape=[jax.ShapeDtypeStruct((part, hid_local), BF16)] * 3,
        in_specs=[vmem] * 5,
        out_specs=[vmem] * 3,
        compiler_params=pltpu.CompilerParams(vmem_limit_bytes=VMEM_LIMIT),
        cost_estimate=pl.CostEstimate(flops=6 * rows * part * hid_local, bytes_accessed=10_000_000, transcendentals=0),
        name="own_grads",
    )(tokens, grads, weights, counts, acts)


def weight_kernel(order, block, *refs):
    shares = refs[:len(order)]
    there_ref, tails_ref, *parts = refs[len(order):len(order) + 5]
    outs = refs[len(order) + 5:len(order) + 8]
    left, right, bufs, sem = refs[len(order) + 8:]
    part, hid_local = outs[0].shape
    me = lax.axis_index("local")
    rows = len(order) * block
    for b, d in enumerate(order):
        for n in range(3):
            right[n, b * block:(b + 1) * block] = there_ref[pl.ds(pl.multiple_of(n * rows + (me ^ d) * block, block), block)]
    pieces = part // PIECE
    half = len(order) // 2
    for b, ref in enumerate(shares):
        left[0, b * block:(b + 1) * block] = ref[:block]
        left[1, b * block:(b + 1) * block - TAIL] = ref[block:]
        source, first = (there_ref, 3 * rows) if b < half else (tails_ref, 0)
        for i in range(pieces):
            down, across = tail_spot(b % half * pieces + i, hid_local)
            left[1, (b + 1) * block - TAIL:(b + 1) * block, i * PIECE:(i + 1) * PIECE] = (
                source[first + down.start:first + down.stop, across])
    chunk = 896
    copies = []
    for i in range(part // chunk):
        cols = pl.ds(i * chunk, chunk)
        for n, out in enumerate(outs):
            bufs[n, cols] = (dot(left[n // 2, :, cols], right[n], 0, 0) + parts[n][cols].astype(F32)).astype(BF16)
            copies.append(pltpu.make_async_copy(bufs.at[n, cols], out.at[cols], sem.at[i, n]))
            copies[-1].start()
    for copy in copies:
        copy.wait()


def weight_grads(order, block, shares, there, tails, parts):
    part = shares[0].shape[-1]
    hid_local = there.shape[1]
    rows = len(order) * block
    vmem = pl.BlockSpec(memory_space=pltpu.VMEM)
    return pl.pallas_call(
        functools.partial(weight_kernel, order, block),
        out_shape=[jax.ShapeDtypeStruct((part, hid_local), BF16)] * 3,
        in_specs=[vmem] * (5 + len(shares)),
        out_specs=[pl.BlockSpec(memory_space=pltpu.HBM)] * 3,
        scratch_shapes=[pltpu.VMEM((2, rows, part), BF16), pltpu.VMEM((3, rows, hid_local), BF16),
                        pltpu.VMEM((3, part, hid_local), BF16), pltpu.SemaphoreType.DMA((part // 896, 3))],
        compiler_params=pltpu.CompilerParams(vmem_limit_bytes=VMEM_LIMIT),
        cost_estimate=pl.CostEstimate(flops=6 * rows * part * hid_local, bytes_accessed=4_000_000, transcendentals=0),
        name="weight_grads",
    )(*shares, there, tails, *parts)


def collect_kernel(*refs):
    *arrived, kept, came, out = refs
    keep, nodes, width = out.shape
    node = lax.axis_index("node")
    last = (kept[...].astype(F32) + came[...].astype(F32)).astype(BF16)
    stacked = jnp.concatenate([last] + [a[...] for a in arrived], axis=0)
    rows = keep * nodes
    p = lax.broadcasted_iota(jnp.int32, (rows, rows), 0)
    source = (node ^ (p & (nodes - 1))) * keep + (p >> log2(nodes))
    one_hot = jnp.where(source == lax.broadcasted_iota(jnp.int32, (rows, rows), 1), 1.0, 0.0).astype(BF16)
    out[...] = dot(one_hot, stacked, 1, 0).astype(BF16).reshape(out.shape)


def after(value, other):
    return lax.optimization_barrier((value, other))[0]


def add(a, b):
    return (a.astype(F32) + b.astype(F32)).astype(BF16)


def on_device(tokens_in, grad_rows, combine_weights, live_counts, w_gate, w_up, w_down):
    slots, nodes, width = tokens_in.shape[2:]
    replicas, locals_ = lax.axis_size("dp"), lax.axis_size("local")
    assert replicas == 2
    keep = slots // locals_
    tokens, grads, weights, counts = tokens_in[0, 0], grad_rows[0, 0], combine_weights[0, 0].T, live_counts[0]
    order = halving_order(locals_)
    bits = [1 << i for i in range(log2(locals_))]

    def swap_local(value, bit):
        return lax.ppermute(value, "local", [(i, i ^ bit) for i in range(locals_)])

    def swap_dp(value):
        return lax.ppermute(value, "dp", [(0, 1), (1, 0)])

    rows = slots * nodes
    block = rows // locals_
    first, weights = lax.optimization_barrier((share(locals_, tokens, grads, weights, counts), weights))
    first = swap_dp(first)
    acts, own_a, own_b, *send = forward(locals_, tokens, grads, weights, counts, w_gate[0], w_up[0], w_down[0])
    there = swap_dp(acts)

    per = nodes // 2
    hops = hop_order(nodes)
    arrived = [None] * nodes
    low_a, high_a, low_b, high_b = send
    came = [swap_local(v, bits[0]) for v in (high_a, high_b, low_a, low_b)]
    came[0] = after(came[0], first)
    half = own_a.shape[0] // 2
    held = [(add(own_a[:half], came[2]), swap_local(add(own_a[half:], came[0]), bits[1]))]
    parts = own_grads(tokens, grads, weights, counts, after(acts, held[0][0]))
    held.append((add(own_b[:half], came[3]), swap_local(after(add(own_b[half:], came[1]), parts[0]), bits[1])))
    for bit in bits[2:]:
        for g, (mine, other) in enumerate(held):
            half = mine.shape[0] // 2
            held[g] = (add(mine[:half], other[:half]), swap_local(add(mine[half:], other[half:]), bit))
    shares = [after(first, held[0][1])]
    for bit in reversed(bits[1:]):
        shares = shares + [swap_local(v, bit) for v in shares]
    for n, k in enumerate(hops):
        mine, other = (v[n % per * keep:(n % per + 1) * keep] for v in held[n // per])
        if k:
            total = add(mine, other)
            arrived[k] = lax.ppermute(total, "node", [(i, i ^ k) for i in range(nodes)])
        else:
            arrived[0] = (mine, other)
    early = lax.optimization_barrier([arrived[k] for k in hops[:per]])
    for k, value in zip(hops[:per], early):
        arrived[k] = value
    d_tokens = pl.pallas_call(
        collect_kernel,
        out_shape=jax.ShapeDtypeStruct((keep, nodes, width), BF16),
        in_specs=[pl.BlockSpec(memory_space=pltpu.VMEM)] * (nodes + 1),
        out_specs=pl.BlockSpec(memory_space=pltpu.VMEM),
        compiler_params=pltpu.CompilerParams(vmem_limit_bytes=VMEM_LIMIT),
        name="collect",
    )(*arrived[1:], *arrived[0])

    for value in arrived[1:]:
        shares[-1] = after(shares[-1], value)
    shares = shares + [swap_local(v, bits[0]) for v in shares]
    tails = swap_local(there[3 * rows:], bits[0])
    grad_gate, grad_up, grad_down = weight_grads(order, block, shares, there, tails, parts)
    return d_tokens[None, None], grad_gate[None], grad_up[None], grad_down[None]


def solution(mesh):
    return jax.shard_map(
        on_device,
        mesh=mesh,
        in_specs=(
            P("dp", "node", None, None, None),
            P("dp", "node", None, None, None),
            P("dp", "node", None, None),
            P("dp", "node", None),
            P("node", None, "local"),
            P("node", None, "local"),
            P("node", None, "local"),
        ),
        out_specs=(
            P("dp", "node", "local", None, None),
            P("node", "dp", "local"),
            P("node", "dp", "local"),
            P("node", "dp", "local"),
        ),
        check_vma=False,
    )
```
